256 devices in a mesh: span: 64 (over y, z_lo, x), depth: 4 (over z_hi, core).
Axes of the slice: x: 4, y: 4, z: 8 (z_hi: 2, z_lo: 4; z = z_hi * 4 + z_lo), core: 2. Of those that a mesh axis runs over, the one named last changes fastest.
Arguments:
- shell_temp: float32 [64, 1024, 256], P('span', 'depth'), may hold values from -6 to 6
- contact_gain: float32 [64, 1024, 256], P('span', 'depth'), may hold values from 0.2 to 2
- die_temp: float32 [48, 2048, 1024], P(None, 'span', 'depth'), may hold values from -4 to 4
- diffusivity: float32 [48, 2048, 1024], P(None, 'span', 'depth'), may hold values from 0.02 to 0.12
- routes: int32 [64, 1024, 1], P('span', 'depth'), may hold values from 0 to 63; in each aligned block of 256 rows (0 to 255, 256 to 511, ..., all dimensions but the last counted through in order) at most 8 rows name the same one
- tile_rows: int32 [64, 1024], P('span', 'depth'), may hold values from 0 to 31
- closed: int32 [64, 1024], P('span', 'depth'), may hold values 0 or 1
Outputs:
- shell_next: float32 [64, 1024, 256], P('span', 'depth')
- die_next: float32 [48, 2048, 1024], P(None, 'span', 'depth')
The draws below stay inside these ranges and needn't reach their ends.
Inputs may be any that keep to these rules, and one draw needn't show every extreme that they name: `routes`: among the 256 block rows of one device, at most 8 name the same span index, and in some device's rows one span index is named exactly 8 times.
All inputs are finite; a program needn't handle non-finite values. No bound on the sum of `closed` on one device may be relied on, other than what follows from the above.
Results may differ from the reference program's by a relative error of at most 0.00025.
Values sent between devices are 32-bit elements; how exact they have to be, the bound alone decides.
No kernel may reach another device: no remote copies, remote signals or barrier semaphores. Data moves between devices by JAX's collectives and lax.ppermute only.
A program may use at most 128 MiB of HBM per device.

```python
import math
import jax
import jax.numpy as jnp
import numpy as np

NB = 256
SB = 256
CX = 32
DZ = 48
CAP = 8
ROWS = 1024
NX = 2048
NY = 1024
N_SPAN = 64
N_DEPTH = 4


def with_ends(values, key, least, top_value):
    longest = values.shape.index(max(values.shape))
    spots = []
    for shift in (0, 1):
        where = [jax.random.randint(jax.random.fold_in(key, axis), (), 0, length) for axis, length in enumerate(values.shape)]
        where[longest] = (where[longest] + shift) % values.shape[longest]
        spots.append(tuple(where))
    return values.at[spots[0]].set(least).at[spots[1]].set(top_value)


def shard_levels(own_key, dims, split, least, largest):
    def one(dim, blocks):
        draws = jax.random.uniform(jax.random.fold_in(jax.random.fold_in(own_key, 6), dim), (blocks,), jnp.float32, least / len(split), largest / len(split))
        return jnp.repeat(jnp.exp(draws), dims[dim] // blocks).reshape((-1,) + (1,) * (len(dims) - dim - 1))

    level = one(*split[0])
    for cut in split[1:]:
        level = level * one(*cut)
    return level


def shared_out(stream_key, own, number, rows, amount, top, limit, lean):
    sequence = jax.random.permutation(stream_key, amount)
    heavy_load, usual = shares(amount, rows * top, limit, lean, True), shares(amount, rows * top, limit, lean, False)
    places = jnp.arange(amount)

    def named(sizes, rotation):
        used = int((sizes > 0).sum())
        fixed = max(1, used // 4)
        shifted = fixed + (places - fixed + rotation * (used - fixed)) % max(1, amount - fixed)
        return jnp.zeros((amount,), jnp.int32).at[sequence[jnp.where(places < fixed, places, shifted)]].set(jnp.asarray(sizes, jnp.int32))

    sizes = jnp.where(number % 4 == 0, named(heavy_load, number // 4), named(usual, number - number // 4 - 1))
    mixed = jax.random.permutation(jax.random.fold_in(own, 3), amount)
    donor, taker = mixed[0:amount // 2 * 2:2], mixed[1:amount // 2 * 2:2]
    slack = jnp.minimum(sizes[donor] - 1, limit - sizes[taker]) // 2
    slack = jnp.where((donor == sequence[0]) | (taker == sequence[0]) | (sizes[taker] == 0), 0, jnp.maximum(slack, 0))
    shifted = jax.random.randint(jax.random.fold_in(own, 4), (amount // 2,), 0, 1 << 20) % (slack + 1)
    sizes = sizes.at[donor].add(-shifted).at[taker].add(shifted)
    members = jnp.searchsorted(jnp.cumsum(sizes), jnp.arange(rows * top), side="right").astype(jnp.int32)
    grid = members.reshape(top, rows).T
    grid = grid[jax.random.permutation(jax.random.fold_in(own, 1), rows)]
    rotation = jax.random.randint(jax.random.fold_in(own, 2), (rows, 1), 0, top)
    return jnp.take_along_axis(grid, (jnp.arange(top)[None, :] + rotation) % top, axis=1)


def shares(amount, total, most, skew, full):
    portions = [(1 << 20) // math.isqrt(grade ** skew) + 1 for grade in range(1, amount + 1)]
    largest = most if full else min(most, max(-(-total // amount), total * portions[0] // sum(portions)))
    least = 1 if total - largest >= amount - 1 else 0
    holding, spare = [largest] + [least] * (amount - 1), total - largest - least * (amount - 1)
    while spare > 0:
        free = [i for i in range(1, amount) if holding[i] < largest] or [i for i in range(1, amount) if holding[i] < most]
        mass, remaining = sum([portions[i] for i in free]), spare
        for i in free:
            addition = min(most - holding[i], max(1, remaining * portions[i] // mass), spare)
            holding[i] = holding[i] + addition
            spare = spare - addition
    return np.array(holding)


def centred(own_key, dims, scale, most, shards=(), held_as=jnp.bfloat16):
    drawn = jax.random.normal(own_key, dims, jnp.float32) * scale
    if len(shards) > 0:
        drawn = shard_levels(own_key, dims, shards, -0.22, 0.18) * drawn
    return jnp.clip(drawn, min=-most, max=most).astype(held_as)


def setup_inputs(seed: int = 0) -> dict:
    keys = jax.random.split(jax.random.key(seed), 8)
    shell_temp = centred(keys[0], (N_SPAN, ROWS, SB), 1.0, 6.0, ((0, 64), (1, 4)), jnp.float32)
    contact_gain = jnp.clip(jnp.exp(math.log(2.0) - 2.3025851 * jax.random.uniform(keys[1], (N_SPAN, ROWS, SB), jnp.float32) ** shard_levels(keys[1], (N_SPAN, ROWS, SB), ((0, 64), (1, 4)), -0.2, 0.2)), 0.2, 2.0)
    die_temp = centred(keys[2], (DZ, NX, NY), 0.5, 4.0, ((1, 64), (2, 4)), jnp.float32)
    diffusivity = jnp.clip(jnp.exp(math.log(0.12) - 1.7917595 * jax.random.uniform(keys[3], (DZ, NX, NY), jnp.float32) ** shard_levels(keys[3], (DZ, NX, NY), ((1, 64), (2, 4)), -0.2, 0.2)), 0.02, 0.12)
    routes_keys = jax.random.split(jax.random.fold_in(keys[4], 1), N_SPAN * ROWS // NB)
    routes_turns = jax.random.permutation(jax.random.fold_in(keys[4], 3), N_SPAN * ROWS // NB)
    routes = jax.vmap(lambda own, number: shared_out(jax.random.fold_in(keys[4], 2), own, number, NB, N_SPAN, 1, CAP, 2))(routes_keys, routes_turns).reshape((N_SPAN, ROWS, 1))
    tile_rows = with_ends(jax.random.randint(keys[5], (N_SPAN, ROWS), 0, CX), jax.random.fold_in(keys[5], 1), 0, CX - 1).astype(jnp.int32)
    closed = with_ends((jax.random.randint(keys[6], (N_SPAN, ROWS), 0, 4) < 3).astype(jnp.int32), jax.random.fold_in(keys[6], 1), 0, 1)
    return dict(shell_temp=shell_temp, contact_gain=contact_gain, die_temp=die_temp, diffusivity=diffusivity, routes=routes, tile_rows=tile_rows, closed=closed)


STENCIL_WEIGHT = (0.0, 1.0, 0.5, 0.25)
SHELL_RATE = 0.15
SHELL_SINK = 0.5
FACE_GAIN = 0.5


def stencil_apply(padded):
    depth_count = padded.shape[0]
    rows_inner = padded.shape[1] - 2
    cols_inner = padded.shape[2] - 2
    framed = jnp.pad(padded, ((1, 1), (0, 0), (0, 0)))
    summed = -14.0 * padded[:, 1:-1, 1:-1]
    for step_z in range(3):
        for step_x in range(3):
            for step_y in range(3):
                reach_count = abs(step_z - 1) + abs(step_x - 1) + abs(step_y - 1)
                if reach_count > 0:
                    summed = summed + STENCIL_WEIGHT[reach_count] * framed[step_z:step_z + depth_count, step_x:step_x + rows_inner, step_y:step_y + cols_inner]
    return summed


def reference(shell_temp, contact_gain, die_temp, diffusivity, routes, tile_rows, closed):
    padded = jnp.pad(shell_temp, ((0, 0), (1, 1), (1, 1)))
    laplace = padded[:, 2:, 1:-1] + padded[:, :-2, 1:-1] + padded[:, 1:-1, 2:] + padded[:, 1:-1, :-2] - 4.0 * shell_temp
    face_row = (routes[:, :, 0] * CX + tile_rows).astype(jnp.int32)
    depth_index = (jnp.arange(ROWS, dtype=jnp.int32) // NB)[None, :]
    face_grid = die_temp[0].reshape(NX, N_DEPTH, SB)
    face_values = face_grid[face_row, depth_index]
    live_mask = closed.astype(jnp.float32)[:, :, None]
    flux = contact_gain * (shell_temp - face_values) * live_mask
    shell_next = shell_temp + SHELL_RATE * laplace - SHELL_SINK * flux
    segment_ids = (face_row * N_DEPTH + depth_index).astype(jnp.int32).reshape(-1)
    heat_in = jax.ops.segment_sum(flux.reshape(-1, SB), segment_ids, num_segments=NX * N_DEPTH).reshape(NX, NY)
    field = die_temp.at[0].add(FACE_GAIN * heat_in)
    for sweep_index in range(2):
        field = field + diffusivity * stencil_apply(jnp.pad(field, ((0, 0), (1, 1), (1, 1))))
    return shell_next, field
```

```python
import jax
import jax.numpy as jnp
from jax import lax
from jax.experimental import pallas as pl
from jax.experimental.pallas import tpu as pltpu
from jax.sharding import PartitionSpec as P

SHELL_RATE = 0.15
SHELL_SINK = 0.5
FACE_GAIN = 0.5
F32 = jnp.float32
BF16 = jnp.bfloat16

NB = 256
SB = 256
CX = 32
DZ = 48
CAP = 8
SPAN = 64
SLOTS = SPAN * CAP
PER = 4 * CAP + 1
EX = CX + 8
EY = SB + 128

VMEM = pl.BlockSpec(memory_space=pltpu.VMEM)


def params(mib):
    return pltpu.CompilerParams(vmem_limit_bytes=mib * 2**20)


def cost(flops, moved):
    return pl.CostEstimate(flops=flops, bytes_accessed=moved, transcendentals=0)


def split3(x):
    hi = x.astype(BF16)
    rest = x - hi.astype(F32)
    mid = rest.astype(BF16)
    low = (rest - mid.astype(F32)).astype(BF16)
    return hi, mid, low


def pick(onehot, x, dims=(((1,), (0,)), ((), ()))):
    total = None
    for part in split3(x):
        term = lax.dot_general(onehot, part, dims, preferred_element_type=F32)
        total = term if total is None else total + term
    return total


def iota(shape, dim):
    return lax.broadcasted_iota(jnp.int32, shape, dim)


def as_column(row, eye):
    return jnp.sum(jnp.where(eye, row, 0.0), axis=1, keepdims=True)


def pack_kernel(routes_ref, tile_ref, closed_ref, temp_ref, gain_ref, out_ref):
    sub, lane = iota((NB, NB), 0), iota((NB, NB), 1)
    eye = sub == lane
    target = routes_ref[...].astype(F32)
    same = as_column(target, eye) == target
    rank_row = jnp.sum(
        jnp.where(jnp.logical_and(same, sub < lane), 1.0, 0.0), axis=0, keepdims=True
    )
    rank_col = jnp.sum(
        jnp.where(jnp.logical_and(same, lane < sub), 1.0, 0.0), axis=1, keepdims=True
    )
    tile_col = as_column(tile_ref[...].astype(F32), eye)
    closed_col = as_column(closed_ref[...].astype(F32), eye)
    position = (target * CAP + rank_row).astype(jnp.int32)
    put = jnp.where(iota((SLOTS, NB), 0) == position, 1.0, 0.0).astype(BF16)
    codes = lax.dot_general(
        jnp.where(iota((SPAN, NB), 0) == routes_ref[...], 1.0, 0.0).astype(BF16),
        jnp.where(iota((NB, 128), 1) == rank_col.astype(jnp.int32), tile_col, 0.0).astype(BF16),
        (((1,), (0,)), ((), ())),
        preferred_element_type=F32,
    )
    out_ref[pl.ds(4 * CAP, SPAN, stride=PER), :] = codes
    temp = pick(put, temp_ref[...])
    gain = pick(put, gain_ref[...] * closed_col)
    for c, slots in enumerate((temp[:, :128], temp[:, 128:], gain[:, :128], gain[:, 128:])):
        for t in range(SPAN):
            out_ref[pl.ds(t * PER + c, CAP, stride=4), :] = slots[t * CAP : (t + 1) * CAP]


def edge_rows_kernel(die_ref, diff_ref, even_ref, odd_ref):
    is_even = lax.rem(lax.axis_index("span"), 2) == 0

    def layer(z, carry):
        for n, (ref, low, high) in enumerate(
            ((die_ref, 0, CX - 2), (die_ref, 1, CX - 1), (diff_ref, 0, CX - 1))
        ):
            first = ref[pl.ds(z * CX + low, 1), :]
            last = ref[pl.ds(z * CX + high, 1), :]
            even_ref[pl.ds(n * DZ + z, 1), :] = jnp.where(is_even, last, first)
            odd_ref[pl.ds(n * DZ + z, 1), :] = jnp.where(is_even, first, last)
        return carry

    lax.fori_loop(0, DZ, layer, 0, unroll=4)


def edge_columns_kernel(
    die_ref, diff_ref, even_in, odd_in, temp_ref, even_ref, odd_ref, die_rim, diff_rim
):
    span_even = lax.rem(lax.axis_index("span"), 2) == 0
    depth_even = lax.rem(lax.axis_index("depth"), 2) == 0
    sub = iota((8, SB), 0)

    def rim_of(z, spots):
        tile = jnp.zeros((8, SB), F32)
        for spot, n, up in spots:
            at = pl.ds(n * DZ + z, 1)
            row = jnp.where(span_even != up, even_in[at, :], odd_in[at, :])
            tile = jnp.where(sub == spot, row, tile)
        return tile

    lane = iota((EX, 128), 1)

    def add_layer(z, kept):
        v_left, v_right, k_left, k_right = kept
        rows, rim = pl.ds(pl.multiple_of(z * CX, CX), CX), pl.ds(pl.multiple_of(z * 8, 8), 8)
        v_rim = rim_of(z, ((0, 0, False), (1, 1, False), (6, 0, True), (7, 1, True)))
        k_rim = rim_of(z, ((0, 2, False), (7, 2, True)))
        die_rim[rim, :] = v_rim
        diff_rim[rim, :] = k_rim
        v = jnp.concatenate([die_ref[rows, :], v_rim], axis=0)
        k = jnp.concatenate([diff_ref[rows, :], k_rim], axis=0)
        v_here, k_here = lax.shift_right_logical(lane, 1) == z, lane == z
        v_left = jnp.where(v_here, pltpu.roll(v[:, :128], 2 * z, 1), v_left)
        v_right = jnp.where(v_here, pltpu.roll(v[:, 128:], 2 * z + 2, 1), v_right)
        k_left = jnp.where(k_here, pltpu.roll(k[:, :128], z, 1), k_left)
        k_right = jnp.where(k_here, pltpu.roll(k[:, 128:], z + 1, 1), k_right)
        return v_left, v_right, k_left, k_right

    none = jnp.zeros((EX, 128), F32)
    v_left, v_right, k_left, k_right = lax.fori_loop(0, DZ, add_layer, (none,) * 4)
    even_ref[:EX, :128] = jnp.where(depth_even, v_right, v_left)
    even_ref[:EX, 128:] = jnp.where(depth_even, k_right, k_left)
    odd_ref[:EX, :128] = jnp.where(depth_even, v_left, v_right)
    odd_ref[:EX, 128:] = jnp.where(depth_even, k_left, k_right)
    first, last = temp_ref[0:1, :], temp_ref[NB - 1 : NB, :]
    even_ref[EX:, :] = jnp.broadcast_to(jnp.where(depth_even, last, first), (8, SB))
    odd_ref[EX:, :] = jnp.broadcast_to(jnp.where(depth_even, first, last), (8, SB))


def across(p):
    q = p + 0.5 * (pltpu.roll(p, 1, 1) + pltpu.roll(p, p.shape[1] - 1, 1))
    return q + 0.5 * (pltpu.roll(q, 1, 0) + pltpu.roll(q, q.shape[0] - 1, 0))


def sweeps_kernel(
    die_ref, diff_ref, die_rim, diff_rim, even_in, odd_in, out_ref, top_ref, field, later, rate
):
    depth_even = lax.rem(lax.axis_index("depth"), 2) == 0
    none = jnp.zeros((EX, EY), F32)
    for ref in (field, later):
        ref[0] = none
        ref[DZ + 1] = none
    lane = iota((EX, 128), 1)

    def fill(z, carry):
        rows, rim = pl.ds(pl.multiple_of(z * CX, CX), CX), pl.ds(pl.multiple_of(z * 8, 8), 8)
        right = jnp.where(depth_even, even_in[:EX, :], odd_in[:EX, :])
        left = jnp.where(depth_even, odd_in[:EX, :], even_in[:EX, :])
        field[z + 1, :CX, :SB] = die_ref[rows, :]
        field[z + 1, CX:, :SB] = die_rim[rim, :]
        rate[z, :CX, :SB] = diff_ref[rows, :]
        rate[z, CX:, :SB] = diff_rim[rim, :]
        v_right = pltpu.roll(right[:, :128], lax.rem(128 - 2 * z, 128), 1)
        v_left = pltpu.roll(left[:, :128], 126 - 2 * z, 1)
        k_right = pltpu.roll(right[:, 128:], lax.rem(128 - z, 128), 1)
        k_left = pltpu.roll(left[:, 128:], 127 - z, 1)
        field[z + 1, :, SB:] = jnp.where(lane < 2, v_right, jnp.where(lane >= 126, v_left, 0.0))
        rate[z, :, SB:] = jnp.where(lane < 1, k_right, jnp.where(lane >= 127, k_left, 0.0))
        return carry

    lax.fori_loop(0, DZ, fill, 0)

    def first(z, carry):
        v = field[z + 1]
        p = 2.0 * v + (field[z] + field[z + 2])
        later[z + 1] = v + rate[z] * (across(p) - 16.0 * v)
        return carry

    lax.fori_loop(0, DZ, first, 0)

    def second(z, carry):
        p = 2.0 * later[z + 1] + (later[z] + later[z + 2])
        q = across(p)[:CX, :SB]
        v = later[z + 1, :CX, :SB]
        out_ref[z] = v + rate[z, :CX, :SB] * (q - 16.0 * v)
        return carry

    lax.fori_loop(0, DZ, second, 0)
    top_ref[...] = rate[0:3]


def owner_kernel(got_ref, face_ref, flux_ref, heat_ref, even_ref, odd_ref):
    codes = got_ref[pl.ds(4 * CAP, SPAN, stride=PER), :]
    lane = iota((SPAN, 128), 1).astype(F32)
    onehot = jnp.concatenate(
        [jnp.where(codes[:, k : k + 1] == lane, 1.0, 0.0) for k in range(CAP)], axis=0
    ).astype(BF16)
    face = face_ref[...]
    padded = jnp.concatenate([face, jnp.zeros((128 - CX, SB), F32)], axis=0)
    touched = pick(onehot, padded)

    def slots(c):
        return jnp.concatenate(
            [got_ref[pl.ds(k * 4 + c, SPAN, stride=PER), :] for k in range(CAP)], axis=0
        )

    temp = jnp.concatenate([slots(0), slots(1)], axis=1)
    gain = jnp.concatenate([slots(2), slots(3)], axis=1)
    flux = gain * (temp - touched)
    for k in range(CAP):
        for c in range(2):
            flux_ref[pl.ds(c * CAP + k, SPAN, stride=2 * CAP), :] = flux[
                k * SPAN : (k + 1) * SPAN, c * 128 : (c + 1) * 128
            ]
    heat = FACE_GAIN * pick(onehot, flux, (((0,), (0,)), ((), ())))[:CX]
    heat_ref[...] = heat
    is_even = lax.rem(lax.axis_index("span"), 2) == 0
    even_ref[...] = jnp.where(is_even, heat[CX - 8 :], heat[:8])
    odd_ref[...] = jnp.where(is_even, heat[:8], heat[CX - 8 :])


def heat_edges_kernel(heat_ref, even_in, odd_in, rows_ref, even_ref, odd_ref):
    span_even = lax.rem(lax.axis_index("span"), 2) == 0
    depth_even = lax.rem(lax.axis_index("depth"), 2) == 0
    below = jnp.where(span_even, even_in[...], odd_in[...])
    above = jnp.where(span_even, odd_in[...], even_in[...])
    sub = iota((8, SB), 0)
    rim = jnp.where(sub < 2, below, jnp.where(sub >= 6, above, 0.0))
    rows = jnp.concatenate([heat_ref[...], rim], axis=0)
    rows_ref[...] = rows
    even_ref[...] = jnp.where(depth_even, rows[:, 128:], rows[:, :128])
    odd_ref[...] = jnp.where(depth_even, rows[:, :128], rows[:, 128:])


def heat_kernel(base_ref, rate_ref, rows_ref, even_in, odd_in, out_ref):
    depth_even = lax.rem(lax.axis_index("depth"), 2) == 0
    right = jnp.where(depth_even, even_in[...], odd_in[...])
    left = jnp.where(depth_even, odd_in[...], even_in[...])
    lane = iota((EX, 128), 1)
    rim = jnp.where(lane < 2, right, jnp.where(lane >= 126, left, 0.0))
    heat = jnp.concatenate([rows_ref[...], rim], axis=1)
    spread = across(heat)
    first = heat + rate_ref[0] * (2.0 * spread - 16.0 * heat)
    second = rate_ref[1] * spread
    for z, (own, p) in enumerate(
        ((first, 2.0 * first + second), (second, 2.0 * second + first), (None, second))
    ):
        step = across(p)
        if own is not None:
            step = step - 16.0 * own
        step = rate_ref[z] * step
        if own is not None:
            step = own + step
        out_ref[z] = base_ref[z] + step[:CX, :SB]


def shell_kernel(routes_ref, temp_ref, even_in, odd_in, base_ref, take_ref):
    depth_even = lax.rem(lax.axis_index("depth"), 2) == 0
    below = jnp.where(depth_even, even_in[EX : EX + 1, :], odd_in[EX : EX + 1, :])
    above = jnp.where(depth_even, odd_in[EX : EX + 1, :], even_in[EX : EX + 1, :])
    temp = temp_ref[...]
    sub, lane = iota((NB, SB), 0), iota((NB, SB), 1)
    upper = jnp.where(sub == 0, above, pltpu.roll(temp, 1, 0))
    lower = jnp.where(sub == NB - 1, below, pltpu.roll(temp, NB - 1, 0))
    before = jnp.where(lane == 0, 0.0, pltpu.roll(temp, 1, 1))
    after = jnp.where(lane == SB - 1, 0.0, pltpu.roll(temp, SB - 1, 1))
    laplace = lower + upper + after + before - 4.0 * temp
    base_ref[...] = temp + SHELL_RATE * laplace
    target = routes_ref[...].astype(F32)
    target_col = as_column(target, sub == lane)
    same = jnp.logical_and(target_col == target, lane < sub)
    rank_col = jnp.sum(jnp.where(same, 1.0, 0.0), axis=1, keepdims=True)
    position = (target_col * CAP + rank_col).astype(jnp.int32)
    take_ref[...] = jnp.where(iota((NB, SLOTS), 1) == position, 1.0, 0.0).astype(BF16)


def sink_kernel(base_ref, take_ref, flux_ref, out_ref):
    take = take_ref[...]
    for c in range(2):
        flux = flux_ref[:, c * CAP : (c + 1) * CAP, :].reshape(SLOTS, 128)
        half = slice(c * 128, (c + 1) * 128)
        out_ref[:, half] = base_ref[:, half] - SHELL_SINK * pick(take, flux)


def swap(even, odd, axis):
    size = lax.axis_size(axis)
    pairs = [(i, i ^ 1) for i in range(size)]
    shifted = [(i, ((i + 1) ^ 1) - 1) for i in range(1, size - 1)]
    return lax.ppermute(even, axis, pairs), lax.ppermute(odd, axis, shifted)


def local(shell_temp, contact_gain, die_temp, diffusivity, routes, tile_rows, closed):
    temp, gain = shell_temp[0], contact_gain[0]
    target = routes.reshape(1, NB)
    die, diff = die_temp.reshape(DZ * CX, SB), diffusivity.reshape(DZ * CX, SB)
    sent = pl.pallas_call(
        pack_kernel,
        out_shape=jax.ShapeDtypeStruct((SPAN * PER, 128), F32),
        in_specs=[VMEM] * 5,
        out_specs=VMEM,
        compiler_params=params(16),
        name="pack",
    )(target, tile_rows, closed, temp, gain)
    got = lax.all_to_all(
        sent.reshape(SPAN * PER, 1, 128), "span", split_axis=0, concat_axis=0, tiled=True
    ).reshape(SPAN * PER, 128)

    rows = jax.ShapeDtypeStruct((3 * DZ, SB), F32)
    even, odd = pl.pallas_call(
        edge_rows_kernel,
        out_shape=(rows, rows),
        in_specs=[VMEM] * 2,
        out_specs=(VMEM,) * 2,
        compiler_params=params(16),
        name="edge_rows",
    )(die, diff)
    even, odd = swap(even, odd, "span")
    columns, rim = (
        jax.ShapeDtypeStruct((EX + 8, SB), F32),
        jax.ShapeDtypeStruct((DZ * 8, SB), F32),
    )
    even, odd, die_rim, diff_rim = pl.pallas_call(
        edge_columns_kernel,
        out_shape=(columns, columns, rim, rim),
        in_specs=[VMEM] * 5,
        out_specs=(VMEM,) * 4,
        compiler_params=params(16),
        name="edge_columns",
    )(die, diff, even, odd, temp)
    even, odd = swap(even, odd, "depth")
    base, top = pl.pallas_call(
        sweeps_kernel,
        out_shape=(
            jax.ShapeDtypeStruct((DZ, CX, SB), F32),
            jax.ShapeDtypeStruct((3, EX, EY), F32),
        ),
        in_specs=[VMEM] * 6,
        out_specs=(VMEM,) * 2,
        scratch_shapes=[
            pltpu.VMEM((DZ + 2, EX, EY), F32),
            pltpu.VMEM((DZ + 2, EX, EY), F32),
            pltpu.VMEM((DZ, EX, EY), F32),
        ],
        compiler_params=params(28),
        cost_estimate=cost(40 * DZ * EX * EY, 5 * DZ * CX * SB * 4),
        name="sweeps",
    )(die, diff, die_rim, diff_rim, even, odd)
    shell_base, take = pl.pallas_call(
        shell_kernel,
        out_shape=(
            jax.ShapeDtypeStruct((NB, SB), F32),
            jax.ShapeDtypeStruct((NB, SLOTS), BF16),
        ),
        in_specs=[VMEM] * 4,
        out_specs=(VMEM,) * 2,
        compiler_params=params(16),
        name="shell",
    )(target, temp, even, odd)

    got, base, shell_base = lax.optimization_barrier((got, base, shell_base))
    edge = jax.ShapeDtypeStruct((8, SB), F32)
    flux, heat, even, odd = pl.pallas_call(
        owner_kernel,
        out_shape=(
            jax.ShapeDtypeStruct((2 * SLOTS, 128), F32),
            jax.ShapeDtypeStruct((CX, SB), F32),
            edge,
            edge,
        ),
        grid=(1,),
        in_specs=[VMEM, pl.BlockSpec((CX, SB), lambda i: (0, 0))],
        out_specs=(VMEM,) * 4,
        compiler_params=params(16),
        name="owner",
    )(got, die)
    back = lax.all_to_all(flux, "span", split_axis=0, concat_axis=0, tiled=True)
    even, odd = swap(even, odd, "span")
    block = jax.ShapeDtypeStruct((EX, 128), F32)
    heat_rows, even, odd = pl.pallas_call(
        heat_edges_kernel,
        out_shape=(jax.ShapeDtypeStruct((EX, SB), F32), block, block),
        in_specs=[VMEM] * 3,
        out_specs=(VMEM,) * 3,
        compiler_params=params(8),
        name="heat_edges",
    )(heat, even, odd)
    even, odd = swap(even, odd, "depth")
    layers = pl.BlockSpec((3, CX, SB), lambda i: (0, 0, 0))
    die_next = pl.pallas_call(
        heat_kernel,
        grid=(1,),
        out_shape=jax.ShapeDtypeStruct((DZ, CX, SB), F32),
        in_specs=[layers] + [VMEM] * 4,
        out_specs=layers,
        input_output_aliases={0: 0},
        compiler_params=params(8),
        name="heat",
    )(base, top, heat_rows, even, odd)
    shell_next = pl.pallas_call(
        sink_kernel,
        out_shape=jax.ShapeDtypeStruct((NB, SB), F32),
        in_specs=[VMEM] * 3,
        out_specs=VMEM,
        compiler_params=params(16),
        name="sink",
    )(shell_base, take, back.reshape(SPAN, 2 * CAP, 128))
    return shell_next[None], die_next


def solution(mesh):
    placed = (
        P("span", "depth", None),
        P("span", "depth", None),
        P(None, "span", "depth"),
        P(None, "span", "depth"),
        P("span", "depth", None),
        P("span", "depth"),
        P("span", "depth"),
    )
    return jax.shard_map(
        local,
        mesh=mesh,
        in_specs=placed,
        out_specs=(P("span", "depth", None), P(None, "span", "depth")),
        check_vma=False,
    )
```

```python
import jax
import jax.numpy as jnp
from jax import lax
from jax.experimental import pallas as pl
from jax.experimental.pallas import tpu as pltpu
from jax.sharding import PartitionSpec as P

SHELL_RATE = 0.15
SHELL_SINK = 0.5
FACE_GAIN = 0.5
F32 = jnp.float32
BF16 = jnp.bfloat16

NB = 256
SB = 256
CX = 32
DZ = 48
CAP = 8
SPAN = 64
SLOTS = SPAN * CAP
PER = 4 * CAP + 1
EX = CX + 8
EY = SB + 128

CHUNKS = 4

VMEM = pl.BlockSpec(memory_space=pltpu.VMEM)
HBM = pl.BlockSpec(memory_space=pltpu.HBM)
ANY = pl.BlockSpec(memory_space=pl.ANY)


def params(mib):
    return pltpu.CompilerParams(vmem_limit_bytes=mib * 2**20)


def cost(flops, moved):
    return pl.CostEstimate(flops=flops, bytes_accessed=moved, transcendentals=0)


def split3(x):
    hi = x.astype(BF16)
    rest = x - hi.astype(F32)
    mid = rest.astype(BF16)
    low = (rest - mid.astype(F32)).astype(BF16)
    return hi, mid, low


def pick(onehot, x, dims=(((1,), (0,)), ((), ()))):
    total = None
    for part in split3(x):
        term = lax.dot_general(onehot, part, dims, preferred_element_type=F32)
        total = term if total is None else total + term
    return total


def iota(shape, dim):
    return lax.broadcasted_iota(jnp.int32, shape, dim)


def as_column(row, eye):
    return jnp.sum(jnp.where(eye, row, 0.0), axis=1, keepdims=True)


def pack_kernel(
    routes_hbm, tile_hbm, closed_hbm, temp_hbm, gain_hbm, after_hbm, out_hbm,
    routes_ref, tile_ref, closed_ref, temp_ref, gain_ref, out_ref, sems, out_sems,
):
    del after_hbm
    loads = [
        pltpu.make_async_copy(source, target, sems.at[n])
        for n, (source, target) in enumerate(
            (
                (routes_hbm, routes_ref),
                (tile_hbm, tile_ref),
                (closed_hbm, closed_ref),
                (temp_hbm, temp_ref),
                (gain_hbm, gain_ref),
            )
        )
    ]
    for load in loads:
        load.start()
    sub, lane = iota((NB, NB), 0), iota((NB, NB), 1)
    eye = sub == lane
    for load in loads[:3]:
        load.wait()
    target = routes_ref[...].astype(F32)
    same = as_column(target, eye) == target
    rank_row = jnp.sum(
        jnp.where(jnp.logical_and(same, sub < lane), 1.0, 0.0), axis=0, keepdims=True
    )
    rank_col = jnp.sum(
        jnp.where(jnp.logical_and(same, lane < sub), 1.0, 0.0), axis=1, keepdims=True
    )
    tile_col = as_column(tile_ref[...].astype(F32), eye)
    closed_col = as_column(closed_ref[...].astype(F32), eye)
    position = (target * CAP + rank_row).astype(jnp.int32)
    codes = lax.dot_general(
        jnp.where(iota((SPAN, NB), 0) == routes_ref[...], 1.0, 0.0).astype(BF16),
        jnp.where(iota((NB, 128), 1) == rank_col.astype(jnp.int32), tile_col, 0.0).astype(BF16),
        (((1,), (0,)), ((), ())),
        preferred_element_type=F32,
    )
    out_ref[pl.ds(4 * CAP, SPAN, stride=PER), :] = codes
    for load in loads[3:]:
        load.wait()
    parts = split3(jnp.concatenate([temp_ref[...], gain_ref[...] * closed_col], axis=1))
    chunk = SPAN // CHUNKS
    stores = []
    for g in range(CHUNKS):
        first = g * chunk * CAP
        put = jnp.where(iota((chunk * CAP, NB), 0) + first == position, 1.0, 0.0).astype(BF16)
        slots = sum(jnp.dot(put, part, preferred_element_type=F32) for part in parts)
        for c in range(4):
            for t in range(chunk):
                out_ref[pl.ds((g * chunk + t) * PER + c, CAP, stride=4), :] = slots[
                    t * CAP : (t + 1) * CAP, c * 128 : (c + 1) * 128
                ]
        rows = pl.ds(g * chunk * PER, chunk * PER)
        stores.append(pltpu.make_async_copy(out_ref.at[rows], out_hbm.at[rows], out_sems.at[g]))
        stores[-1].start()
    for store in stores:
        store.wait()


def edge_rows_kernel(die_first, die_last, diff_first, diff_last, even_ref, odd_ref):
    is_even = lax.rem(lax.axis_index("span"), 2) == 0

    def layer(z, carry):
        for n, (first, low, last, high) in enumerate(
            ((die_first, 0, die_last, 6), (die_first, 1, die_last, 7), (diff_first, 0, diff_last, 7))
        ):
            top = first[z, low : low + 1, :]
            bottom = last[z, high : high + 1, :]
            even_ref[pl.ds(n * DZ + z, 1), :] = jnp.where(is_even, bottom, top)
            odd_ref[pl.ds(n * DZ + z, 1), :] = jnp.where(is_even, top, bottom)
        return carry

    lax.fori_loop(0, DZ, layer, 0, unroll=8)


def edge_columns_kernel(
    die_ref, diff_ref, even_in, odd_in, temp_ref, even_ref, odd_ref, die_rim, diff_rim
):
    span_even = lax.rem(lax.axis_index("span"), 2) == 0
    depth_even = lax.rem(lax.axis_index("depth"), 2) == 0
    sub = iota((8, SB), 0)

    def rim_of(z, spots):
        tile = jnp.zeros((8, SB), F32)
        for spot, n, up in spots:
            at = pl.ds(n * DZ + z, 1)
            row = jnp.where(span_even != up, even_in[at, :], odd_in[at, :])
            tile = jnp.where(sub == spot, row, tile)
        return tile

    lane = iota((EX, 128), 1)

    def add_layer(z, kept):
        v_left, v_right, k_left, k_right = kept
        rows, rim = pl.ds(pl.multiple_of(z * CX, CX), CX), pl.ds(pl.multiple_of(z * 8, 8), 8)
        v_rim = rim_of(z, ((0, 0, False), (1, 1, False), (6, 0, True), (7, 1, True)))
        k_rim = rim_of(z, ((0, 2, False), (7, 2, True)))
        die_rim[rim, :] = v_rim
        diff_rim[rim, :] = k_rim
        v = jnp.concatenate([die_ref[rows, :], v_rim], axis=0)
        k = jnp.concatenate([diff_ref[rows, :], k_rim], axis=0)
        v_here, k_here = lax.shift_right_logical(lane, 1) == z, lane == z
        v_left = jnp.where(v_here, pltpu.roll(v[:, :128], 2 * z, 1), v_left)
        v_right = jnp.where(v_here, pltpu.roll(v[:, 128:], 2 * z + 2, 1), v_right)
        k_left = jnp.where(k_here, pltpu.roll(k[:, :128], z, 1), k_left)
        k_right = jnp.where(k_here, pltpu.roll(k[:, 128:], z + 1, 1), k_right)
        return v_left, v_right, k_left, k_right

    none = jnp.zeros((EX, 128), F32)
    v_left, v_right, k_left, k_right = lax.fori_loop(0, DZ, add_layer, (none,) * 4, unroll=8)
    even_ref[:EX, :128] = jnp.where(depth_even, v_right, v_left)
    even_ref[:EX, 128:] = jnp.where(depth_even, k_right, k_left)
    odd_ref[:EX, :128] = jnp.where(depth_even, v_left, v_right)
    odd_ref[:EX, 128:] = jnp.where(depth_even, k_left, k_right)
    first, last = temp_ref[0:1, :], temp_ref[NB - 1 : NB, :]
    even_ref[EX:, :] = jnp.broadcast_to(jnp.where(depth_even, last, first), (8, SB))
    odd_ref[EX:, :] = jnp.broadcast_to(jnp.where(depth_even, first, last), (8, SB))


def across(p):
    q = p + 0.5 * (pltpu.roll(p, 1, 1) + pltpu.roll(p, p.shape[1] - 1, 1))
    return q + 0.5 * (pltpu.roll(q, 1, 0) + pltpu.roll(q, q.shape[0] - 1, 0))


def sweeps_kernel(
    die_ref, diff_ref, die_rim, diff_rim, even_in, odd_in, out_ref, top_ref, field, later, rate
):
    depth_even = lax.rem(lax.axis_index("depth"), 2) == 0
    none = jnp.zeros((EX, EY), F32)
    for ref in (field, later):
        ref[0] = none
        ref[DZ + 1] = none
    lane = iota((EX, 128), 1)

    def fill(z, carry):
        rows, rim = pl.ds(pl.multiple_of(z * CX, CX), CX), pl.ds(pl.multiple_of(z * 8, 8), 8)
        right = jnp.where(depth_even, even_in[:EX, :], odd_in[:EX, :])
        left = jnp.where(depth_even, odd_in[:EX, :], even_in[:EX, :])
        field[z + 1, :CX, :SB] = die_ref[rows, :]
        field[z + 1, CX:, :SB] = die_rim[rim, :]
        rate[z, :CX, :SB] = diff_ref[rows, :]
        rate[z, CX:, :SB] = diff_rim[rim, :]
        v_right = pltpu.roll(right[:, :128], lax.rem(128 - 2 * z, 128), 1)
        v_left = pltpu.roll(left[:, :128], 126 - 2 * z, 1)
        k_right = pltpu.roll(right[:, 128:], lax.rem(128 - z, 128), 1)
        k_left = pltpu.roll(left[:, 128:], 127 - z, 1)
        field[z + 1, :, SB:] = jnp.where(lane < 2, v_right, jnp.where(lane >= 126, v_left, 0.0))
        rate[z, :, SB:] = jnp.where(lane < 1, k_right, jnp.where(lane >= 127, k_left, 0.0))
        return carry

    lax.fori_loop(0, DZ, fill, 0, unroll=8)

    def first(z, carry):
        v = field[z + 1]
        p = 2.0 * v + (field[z] + field[z + 2])
        later[z + 1] = v + rate[z] * (across(p) - 16.0 * v)
        return carry

    lax.fori_loop(0, DZ, first, 0, unroll=4)

    def second(z, carry):
        p = 2.0 * later[z + 1] + (later[z] + later[z + 2])
        q = across(p)[:CX, :SB]
        v = later[z + 1, :CX, :SB]
        out_ref[z] = v + rate[z, :CX, :SB] * (q - 16.0 * v)
        return carry

    lax.fori_loop(0, DZ, second, 0, unroll=4)
    top_ref[...] = rate[0:3]


def owner_kernel(got_ref, face_ref, flux_ref, heat_ref, even_ref, odd_ref):
    codes = got_ref[pl.ds(4 * CAP, SPAN, stride=PER), :]
    lane = iota((SPAN, 128), 1).astype(F32)
    onehot = jnp.concatenate(
        [jnp.where(codes[:, k : k + 1] == lane, 1.0, 0.0) for k in range(CAP)], axis=0
    ).astype(BF16)
    face = face_ref[...]
    padded = jnp.concatenate([face, jnp.zeros((128 - CX, SB), F32)], axis=0)
    touched = pick(onehot, padded)

    def slots(c):
        return jnp.concatenate(
            [got_ref[pl.ds(k * 4 + c, SPAN, stride=PER), :] for k in range(CAP)], axis=0
        )

    temp = jnp.concatenate([slots(0), slots(1)], axis=1)
    gain = jnp.concatenate([slots(2), slots(3)], axis=1)
    flux = gain * (temp - touched)
    for k in range(CAP):
        for c in range(2):
            flux_ref[pl.ds(c * CAP + k, SPAN, stride=2 * CAP), :] = flux[
                k * SPAN : (k + 1) * SPAN, c * 128 : (c + 1) * 128
            ]
    heat = FACE_GAIN * pick(onehot, flux, (((0,), (0,)), ((), ())))[:CX]
    heat_ref[...] = heat
    is_even = lax.rem(lax.axis_index("span"), 2) == 0
    even_ref[...] = jnp.where(is_even, heat[CX - 8 :], heat[:8])
    odd_ref[...] = jnp.where(is_even, heat[:8], heat[CX - 8 :])


def heat_edges_kernel(heat_ref, even_in, odd_in, rows_ref, even_ref, odd_ref):
    span_even = lax.rem(lax.axis_index("span"), 2) == 0
    depth_even = lax.rem(lax.axis_index("depth"), 2) == 0
    below = jnp.where(span_even, even_in[...], odd_in[...])
    above = jnp.where(span_even, odd_in[...], even_in[...])
    sub = iota((8, SB), 0)
    rim = jnp.where(sub < 2, below, jnp.where(sub >= 6, above, 0.0))
    rows = jnp.concatenate([heat_ref[...], rim], axis=0)
    rows_ref[...] = rows
    even_ref[...] = jnp.where(depth_even, rows[:, 128:], rows[:, :128])
    odd_ref[...] = jnp.where(depth_even, rows[:, :128], rows[:, 128:])


def heat_kernel(base_ref, rate_ref, rows_ref, even_in, odd_in, out_ref):
    depth_even = lax.rem(lax.axis_index("depth"), 2) == 0
    right = jnp.where(depth_even, even_in[...], odd_in[...])
    left = jnp.where(depth_even, odd_in[...], even_in[...])
    lane = iota((EX, 128), 1)
    rim = jnp.where(lane < 2, right, jnp.where(lane >= 126, left, 0.0))
    heat = jnp.concatenate([rows_ref[...], rim], axis=1)
    spread = across(heat)
    first = heat + rate_ref[0] * (2.0 * spread - 16.0 * heat)
    second = rate_ref[1] * spread
    for z, (own, p) in enumerate(
        ((first, 2.0 * first + second), (second, 2.0 * second + first), (None, second))
    ):
        step = across(p)
        if own is not None:
            step = step - 16.0 * own
        step = rate_ref[z] * step
        if own is not None:
            step = own + step
        out_ref[z] = base_ref[z] + step[:CX, :SB]


def shell_kernel(routes_ref, temp_ref, even_in, odd_in, base_ref, take_ref):
    depth_even = lax.rem(lax.axis_index("depth"), 2) == 0
    below = jnp.where(depth_even, even_in[EX : EX + 1, :], odd_in[EX : EX + 1, :])
    above = jnp.where(depth_even, odd_in[EX : EX + 1, :], even_in[EX : EX + 1, :])
    temp = temp_ref[...]
    sub, lane = iota((NB, SB), 0), iota((NB, SB), 1)
    upper = jnp.where(sub == 0, above, pltpu.roll(temp, 1, 0))
    lower = jnp.where(sub == NB - 1, below, pltpu.roll(temp, NB - 1, 0))
    before = jnp.where(lane == 0, 0.0, pltpu.roll(temp, 1, 1))
    after = jnp.where(lane == SB - 1, 0.0, pltpu.roll(temp, SB - 1, 1))
    laplace = lower + upper + after + before - 4.0 * temp
    base_ref[...] = temp + SHELL_RATE * laplace
    target = routes_ref[...].astype(F32)
    target_col = as_column(target, sub == lane)
    same = jnp.logical_and(target_col == target, lane < sub)
    rank_col = jnp.sum(jnp.where(same, 1.0, 0.0), axis=1, keepdims=True)
    position = (target_col * CAP + rank_col).astype(jnp.int32)
    take_ref[...] = jnp.where(iota((NB, SLOTS), 1) == position, 1.0, 0.0).astype(BF16)


def sink_kernel(base_ref, take_ref, flux_ref, out_ref):
    take = take_ref[...]
    for c in range(2):
        flux = flux_ref[:, c * CAP : (c + 1) * CAP, :].reshape(SLOTS, 128)
        half = slice(c * 128, (c + 1) * 128)
        out_ref[:, half] = base_ref[:, half] - SHELL_SINK * pick(take, flux)


def swap(even, odd, axis):
    size = lax.axis_size(axis)
    pairs = [(i, i ^ 1) for i in range(size)]
    shifted = [(i, ((i + 1) ^ 1) - 1) for i in range(1, size - 1)]
    return lax.ppermute(even, axis, pairs), lax.ppermute(odd, axis, shifted)


def local(shell_temp, contact_gain, die_temp, diffusivity, routes, tile_rows, closed):
    temp, gain = shell_temp[0], contact_gain[0]
    target = routes.reshape(1, NB)
    die, diff = die_temp.reshape(DZ * CX, SB), diffusivity.reshape(DZ * CX, SB)
    rows = jax.ShapeDtypeStruct((3 * DZ, SB), F32)
    even, odd = pl.pallas_call(
        edge_rows_kernel,
        out_shape=(rows, rows),
        grid=(1,),
        in_specs=[
            pl.BlockSpec((DZ, 8, SB), lambda i: (0, 0, 0)),
            pl.BlockSpec((DZ, 8, SB), lambda i: (0, CX // 8 - 1, 0)),
        ]
        * 2,
        out_specs=(VMEM,) * 2,
        compiler_params=params(60),
        name="edge_rows",
    )(die_temp, die_temp, diffusivity, diffusivity)
    sent = pl.pallas_call(
        pack_kernel,
        out_shape=jax.ShapeDtypeStruct((SPAN * PER, 128), F32),
        in_specs=[HBM] * 5 + [ANY],
        out_specs=HBM,
        scratch_shapes=[
            pltpu.VMEM((1, NB), jnp.int32),
            pltpu.VMEM((1, NB), jnp.int32),
            pltpu.VMEM((1, NB), jnp.int32),
            pltpu.VMEM((NB, SB), F32),
            pltpu.VMEM((NB, SB), F32),
            pltpu.VMEM((SPAN * PER, 128), F32),
            pltpu.SemaphoreType.DMA((5,)),
            pltpu.SemaphoreType.DMA((CHUNKS,)),
        ],
        compiler_params=params(60),
        cost_estimate=cost(6 * SLOTS * NB * 2 * SB, 4 * 2**20),
        name="pack",
    )(target, tile_rows, closed, temp, gain, even)
    even, odd = swap(even, odd, "span")
    got = lax.all_to_all(
        sent.reshape(SPAN * PER, 1, 128), "span", split_axis=0, concat_axis=0, tiled=True
    ).reshape(SPAN * PER, 128)
    columns, rim = (
        jax.ShapeDtypeStruct((EX + 8, SB), F32),
        jax.ShapeDtypeStruct((DZ * 8, SB), F32),
    )
    even, odd, die_rim, diff_rim = pl.pallas_call(
        edge_columns_kernel,
        out_shape=(columns, columns, rim, rim),
        in_specs=[VMEM] * 5,
        out_specs=(VMEM,) * 4,
        compiler_params=params(16),
        cost_estimate=cost(10**12, 2**32),
        name="edge_columns",
    )(die, diff, even, odd, temp)
    even, odd = swap(even, odd, "depth")
    base, top = pl.pallas_call(
        sweeps_kernel,
        out_shape=(
            jax.ShapeDtypeStruct((DZ, CX, SB), F32),
            jax.ShapeDtypeStruct((3, EX, EY), F32),
        ),
        in_specs=[VMEM] * 6,
        out_specs=(VMEM,) * 2,
        scratch_shapes=[
            pltpu.VMEM((DZ + 2, EX, EY), F32),
            pltpu.VMEM((DZ + 2, EX, EY), F32),
            pltpu.VMEM((DZ, EX, EY), F32),
        ],
        compiler_params=params(20),
        cost_estimate=cost(40 * DZ * EX * EY, 5 * DZ * CX * SB * 4),
        name="sweeps",
    )(die, diff, die_rim, diff_rim, even, odd)
    shell_base, take = pl.pallas_call(
        shell_kernel,
        out_shape=(
            jax.ShapeDtypeStruct((NB, SB), F32),
            jax.ShapeDtypeStruct((NB, SLOTS), BF16),
        ),
        in_specs=[VMEM] * 4,
        out_specs=(VMEM,) * 2,
        compiler_params=params(16),
        name="shell",
    )(target, temp, even, odd)

    got, base, shell_base = lax.optimization_barrier((got, base, shell_base))
    edge = jax.ShapeDtypeStruct((8, SB), F32)
    flux, heat, even, odd = pl.pallas_call(
        owner_kernel,
        out_shape=(
            jax.ShapeDtypeStruct((2 * SLOTS, 128), F32),
            jax.ShapeDtypeStruct((CX, SB), F32),
            edge,
            edge,
        ),
        grid=(1,),
        in_specs=[VMEM, pl.BlockSpec((CX, SB), lambda i: (0, 0))],
        out_specs=(VMEM,) * 4,
        compiler_params=params(60),
        name="owner",
    )(got, die)
    back = lax.all_to_all(flux, "span", split_axis=0, concat_axis=0, tiled=True)
    even, odd = swap(even, odd, "span")
    block = jax.ShapeDtypeStruct((EX, 128), F32)
    heat_rows, even, odd = pl.pallas_call(
        heat_edges_kernel,
        out_shape=(jax.ShapeDtypeStruct((EX, SB), F32), block, block),
        in_specs=[VMEM] * 3,
        out_specs=(VMEM,) * 3,
        compiler_params=params(8),
        cost_estimate=cost(10**12, 2**32),
        name="heat_edges",
    )(heat, even, odd)
    even, odd = swap(even, odd, "depth")
    layers = pl.BlockSpec((3, CX, SB), lambda i: (0, 0, 0))
    die_next = pl.pallas_call(
        heat_kernel,
        grid=(1,),
        out_shape=jax.ShapeDtypeStruct((DZ, CX, SB), F32),
        in_specs=[layers] + [VMEM] * 4,
        out_specs=layers,
        input_output_aliases={0: 0},
        compiler_params=params(8),
        name="heat",
    )(base, top, heat_rows, even, odd)
    shell_next = pl.pallas_call(
        sink_kernel,
        out_shape=jax.ShapeDtypeStruct((NB, SB), F32),
        in_specs=[VMEM] * 3,
        out_specs=VMEM,
        compiler_params=params(16),
        name="sink",
    )(shell_base, take, back.reshape(SPAN, 2 * CAP, 128))
    return shell_next[None], die_next


def solution(mesh):
    placed = (
        P("span", "depth", None),
        P("span", "depth", None),
        P(None, "span", "depth"),
        P(None, "span", "depth"),
        P("span", "depth", None),
        P("span", "depth"),
        P("span", "depth"),
    )
    return jax.shard_map(
        local,
        mesh=mesh,
        in_specs=placed,
        out_specs=(P("span", "depth", None), P(None, "span", "depth")),
        check_vma=False,
    )
```

```python
import jax
import jax.numpy as jnp
from jax import lax
from jax.experimental import pallas as pl
from jax.experimental.pallas import tpu as pltpu
from jax.sharding import PartitionSpec as P

SHELL_RATE = 0.15
SHELL_SINK = 0.5
FACE_GAIN = 0.5
F32 = jnp.float32
BF16 = jnp.bfloat16

NB = 256
SB = 256
CX = 32
DZ = 48
CAP = 8
SPAN = 64
SLOTS = SPAN * CAP
PER = 4 * CAP + 1
EX = CX + 8
EY = SB + 128

CHUNKS = 4
UNROLL = 3
GROUP = 4

VMEM = pl.BlockSpec(memory_space=pltpu.VMEM)
HBM = pl.BlockSpec(memory_space=pltpu.HBM)
ANY = pl.BlockSpec(memory_space=pl.ANY)


def whole(*shape):
    return pl.BlockSpec(shape, lambda i: (0,) * len(shape))


def params(mib):
    return pltpu.CompilerParams(vmem_limit_bytes=mib * 2**20)


def cost(flops, moved):
    return pl.CostEstimate(flops=flops, bytes_accessed=moved, transcendentals=0)


def split(x):
    high = x.astype(BF16)
    return high, (x - high.astype(F32)).astype(BF16)


def pick(onehot, x, dims=(((1,), (0,)), ((), ()))):
    total = None
    for part in split(x):
        term = lax.dot_general(onehot, part, dims, preferred_element_type=F32)
        total = term if total is None else total + term
    return total


def iota(shape, dim):
    return lax.broadcasted_iota(jnp.int32, shape, dim)


def as_column(row, eye):
    return jnp.sum(jnp.where(eye, row, 0.0), axis=1, keepdims=True)


def pack_kernel(
    routes_hbm, tile_hbm, closed_hbm, temp_hbm, gain_hbm, out_hbm,
    routes_ref, tile_ref, closed_ref, temp_ref, gain_ref, out_ref, sems, out_sems,
):
    loads = [
        pltpu.make_async_copy(source, target, sems.at[n])
        for n, (source, target) in enumerate(
            (
                (routes_hbm, routes_ref),
                (tile_hbm, tile_ref),
                (closed_hbm, closed_ref),
                (temp_hbm, temp_ref),
                (gain_hbm, gain_ref),
            )
        )
    ]
    for load in loads:
        load.start()
    sub, lane = iota((NB, NB), 0), iota((NB, NB), 1)
    eye = sub == lane
    for load in loads[:3]:
        load.wait()
    target = routes_ref[...].astype(F32)
    same = as_column(target, eye) == target
    rank_row = jnp.sum(
        jnp.where(jnp.logical_and(same, sub < lane), 1.0, 0.0), axis=0, keepdims=True
    )
    rank_col = jnp.sum(
        jnp.where(jnp.logical_and(same, lane < sub), 1.0, 0.0), axis=1, keepdims=True
    )
    tile_col = as_column(tile_ref[...].astype(F32), eye)
    closed_col = as_column(closed_ref[...].astype(F32), eye)
    position = (target * CAP + rank_row).astype(jnp.int32)
    codes = lax.dot_general(
        jnp.where(iota((SPAN, NB), 0) == routes_ref[...], 1.0, 0.0).astype(BF16),
        jnp.where(iota((NB, 128), 1) == rank_col.astype(jnp.int32), tile_col, 0.0).astype(BF16),
        (((1,), (0,)), ((), ())),
        preferred_element_type=F32,
    )
    out_ref[pl.ds(4 * CAP, SPAN, stride=PER), :] = codes
    for load in loads[3:]:
        load.wait()
    parts = split(jnp.concatenate([temp_ref[...], gain_ref[...] * closed_col], axis=1))
    chunk = SPAN // CHUNKS
    stores = []
    for g in range(CHUNKS):
        first = g * chunk * CAP
        put = jnp.where(iota((chunk * CAP, NB), 0) + first == position, 1.0, 0.0).astype(BF16)
        slots = sum(jnp.dot(put, part, preferred_element_type=F32) for part in parts)
        for c in range(4):
            for t in range(chunk):
                out_ref[pl.ds((g * chunk + t) * PER + c, CAP, stride=4), :] = slots[
                    t * CAP : (t + 1) * CAP, c * 128 : (c + 1) * 128
                ]
        rows = pl.ds(g * chunk * PER, chunk * PER)
        stores.append(pltpu.make_async_copy(out_ref.at[rows], out_hbm.at[rows], out_sems.at[g]))
        stores[-1].start()
    for store in stores:
        store.wait()


def edge_rows_kernel(die_first, die_last, diff_first, diff_last, even_ref, odd_ref):
    is_even = lax.rem(lax.axis_index("span"), 2) == 0

    def layer(z, carry):
        for n, (first, low, last, high) in enumerate(
            ((die_first, 0, die_last, 6), (die_first, 1, die_last, 7), (diff_first, 0, diff_last, 7))
        ):
            top = first[z, low : low + 1, :]
            bottom = last[z, high : high + 1, :]
            even_ref[pl.ds(n * DZ + z, 1), :] = jnp.where(is_even, bottom, top)
            odd_ref[pl.ds(n * DZ + z, 1), :] = jnp.where(is_even, top, bottom)
        return carry

    lax.fori_loop(0, DZ, layer, 0, unroll=8)


def edge_columns_kernel(
    die_ref, diff_ref, even_in, odd_in, temp_ref, even_ref, odd_ref, die_rim, diff_rim, face_ref
):
    span_even = lax.rem(lax.axis_index("span"), 2) == 0
    depth_even = lax.rem(lax.axis_index("depth"), 2) == 0
    sub = iota((8, SB), 0)

    def rim_of(z, spots):
        tile = jnp.zeros((8, SB), F32)
        for spot, n, up in spots:
            at = pl.ds(n * DZ + z, 1)
            row = jnp.where(span_even != up, even_in[at, :], odd_in[at, :])
            tile = jnp.where(sub == spot, row, tile)
        return tile

    lane = iota((EX, 128), 1)

    def add_layer(z, kept):
        v_left, v_right, k_left, k_right = kept
        rows, rim = pl.ds(pl.multiple_of(z * CX, CX), CX), pl.ds(pl.multiple_of(z * 8, 8), 8)
        v_rim = rim_of(z, ((0, 0, False), (1, 1, False), (6, 0, True), (7, 1, True)))
        k_rim = rim_of(z, ((0, 2, False), (7, 2, True)))
        die_rim[rim, :] = v_rim
        diff_rim[rim, :] = k_rim
        v = jnp.concatenate([die_ref[rows, :], v_rim], axis=0)
        k = jnp.concatenate([diff_ref[rows, :], k_rim], axis=0)
        v_here, k_here = lax.shift_right_logical(lane, 1) == z, lane == z
        v_left = jnp.where(v_here, pltpu.roll(v[:, :128], 2 * z, 1), v_left)
        v_right = jnp.where(v_here, pltpu.roll(v[:, 128:], 2 * z + 2, 1), v_right)
        k_left = jnp.where(k_here, pltpu.roll(k[:, :128], z, 1), k_left)
        k_right = jnp.where(k_here, pltpu.roll(k[:, 128:], z + 1, 1), k_right)
        return v_left, v_right, k_left, k_right

    none = jnp.zeros((EX, 128), F32)
    v_left, v_right, k_left, k_right = lax.fori_loop(0, DZ, add_layer, (none,) * 4, unroll=8)
    even_ref[:EX, :128] = jnp.where(depth_even, v_right, v_left)
    even_ref[:EX, 128:] = jnp.where(depth_even, k_right, k_left)
    odd_ref[:EX, :128] = jnp.where(depth_even, v_left, v_right)
    odd_ref[:EX, 128:] = jnp.where(depth_even, k_left, k_right)
    first, last = temp_ref[0:1, :], temp_ref[NB - 1 : NB, :]
    even_ref[EX:, :] = jnp.broadcast_to(jnp.where(depth_even, last, first), (8, SB))
    odd_ref[EX:, :] = jnp.broadcast_to(jnp.where(depth_even, first, last), (8, SB))
    face_ref[...] = die_ref[:CX, :]


def across(p):
    q = p + 0.5 * (pltpu.roll(p, 1, 1) + pltpu.roll(p, p.shape[1] - 1, 1))
    return q + 0.5 * (pltpu.roll(q, 1, 0) + pltpu.roll(q, q.shape[0] - 1, 0))


def sweeps_kernel(
    die_hbm, diff_hbm, die_rim, diff_rim, heat_ref, even_in, odd_in, out_hbm,
    die_ref, diff_ref, out_ref, field, later, rate, sems, out_sems,
):
    some = DZ // CHUNKS
    loads = []
    for n in range(CHUNKS):
        for m, (source, target) in enumerate(((die_hbm, die_ref), (diff_hbm, diff_ref))):
            rows = pl.ds(n * some * CX, some * CX)
            loads.append(
                pltpu.make_async_copy(source.at[rows], target.at[rows], sems.at[2 * n + m])
            )
            loads[-1].start()
    depth_even = lax.rem(lax.axis_index("depth"), 2) == 0
    none = jnp.zeros((EX, EY), F32)
    for ref in (field, later):
        ref[0] = none
        ref[DZ + 1] = none
    lane = iota((EX, 128), 1)
    right = jnp.where(depth_even, even_in[:EX, :], odd_in[:EX, :])
    left = jnp.where(depth_even, odd_in[:EX, :], even_in[:EX, :])
    for n in range(CHUNKS):
        loads[2 * n].wait()
        loads[2 * n + 1].wait()
        for z in range(n * some, (n + 1) * some):
            field[z + 1, :CX, :SB] = die_ref[z * CX : (z + 1) * CX, :]
            field[z + 1, CX:, :SB] = die_rim[z * 8 : (z + 1) * 8, :]
            rate[z, :CX, :SB] = diff_ref[z * CX : (z + 1) * CX, :]
            rate[z, CX:, :SB] = diff_rim[z * 8 : (z + 1) * 8, :]
            v_right = pltpu.roll(right[:, :128], (128 - 2 * z) % 128, 1)
            v_left = pltpu.roll(left[:, :128], 126 - 2 * z, 1)
            k_right = pltpu.roll(right[:, 128:], (128 - z) % 128, 1)
            k_left = pltpu.roll(left[:, 128:], 127 - z, 1)
            field[z + 1, :, SB:] = jnp.where(
                lane < 2, v_right, jnp.where(lane >= 126, v_left, 0.0)
            )
            rate[z, :, SB:] = jnp.where(lane < 1, k_right, jnp.where(lane >= 127, k_left, 0.0))
    h_right = pltpu.roll(right[:, :128], 128 - 2 * DZ, 1)
    h_left = pltpu.roll(left[:, :128], 126 - 2 * DZ, 1)
    field[1, :, :SB] += heat_ref[...]
    field[1, :, SB:] += jnp.where(lane < 2, h_right, jnp.where(lane >= 126, h_left, 0.0))

    gap = jnp.abs(iota((EY, EY), 0) - iota((EY, EY), 1))
    band = jnp.where(
        gap == 0, 1.0, jnp.where(jnp.logical_or(gap == 1, gap == EY - 1), 0.5, 0.0)
    ).astype(BF16)

    def around(ref, start, width):
        layers = []
        for n in range(GROUP):
            z = start + n
            layers.append(2.0 * ref[z + 1] + (ref[z] + ref[z + 2]))
        p = jnp.concatenate(layers, axis=0)
        high, low = split(p)
        q = jnp.dot(high, band[:, :width], preferred_element_type=F32)
        q = q + jnp.dot(low, band[:, :width], preferred_element_type=F32)
        for n in range(GROUP):
            own = q[n * EX : (n + 1) * EX]
            yield own + 0.5 * (pltpu.roll(own, 1, 0) + pltpu.roll(own, EX - 1, 0))

    def first(g, carry):
        for n, q in enumerate(around(field, g * GROUP, EY)):
            z = g * GROUP + n
            v = field[z + 1]
            later[z + 1] = v + rate[z] * (q - 16.0 * v)
        return carry

    lax.fori_loop(0, DZ // GROUP, first, 0, unroll=4 * UNROLL)

    def second(g, carry):
        for n, q in enumerate(around(later, g * GROUP, SB)):
            z = g * GROUP + n
            v = later[z + 1, :CX, :SB]
            out_ref[z] = v + rate[z, :CX, :SB] * (q[:CX] - 16.0 * v)
        return carry

    stores = []
    for n in range(CHUNKS):
        lax.fori_loop(
            n * some // GROUP, (n + 1) * some // GROUP, second, 0, unroll=UNROLL
        )
        layers = pl.ds(n * some, some)
        stores.append(pltpu.make_async_copy(out_ref.at[layers], out_hbm.at[layers], out_sems.at[n]))
        stores[-1].start()
    for store in stores:
        store.wait()


def owner_kernel(
    got_hbm, face_ref, flux_hbm, heat_ref, even_ref, odd_ref,
    got_ref, flux_ref, sems, out_sem,
):
    rows = SPAN * PER // CHUNKS
    loads = [
        pltpu.make_async_copy(
            got_hbm.at[pl.ds(n * rows, rows)], got_ref.at[pl.ds(n * rows, rows)], sems.at[n]
        )
        for n in range(CHUNKS)
    ]
    for load in loads:
        load.start()
    lane = iota((SPAN, 128), 1).astype(F32)
    faces = jnp.concatenate([face_ref[...], jnp.zeros((128 - CX, SB), F32)], axis=0)
    for load in loads:
        load.wait()
    codes = got_ref[pl.ds(4 * CAP, SPAN, stride=PER), :]
    onehot = jnp.concatenate(
        [jnp.where(codes[:, k : k + 1] == lane, 1.0, 0.0) for k in range(CAP)], axis=0
    ).astype(BF16)
    touched = pick(onehot, faces)

    def slots(c):
        return jnp.concatenate(
            [got_ref[pl.ds(k * 4 + c, SPAN, stride=PER), :] for k in range(CAP)], axis=0
        )

    temp = jnp.concatenate([slots(0), slots(1)], axis=1)
    gain = jnp.concatenate([slots(2), slots(3)], axis=1)
    flux = gain * (temp - touched)
    for k in range(CAP):
        for c in range(2):
            flux_ref[pl.ds(c * CAP + k, SPAN, stride=2 * CAP), :] = flux[
                k * SPAN : (k + 1) * SPAN, c * 128 : (c + 1) * 128
            ]
    store = pltpu.make_async_copy(flux_ref, flux_hbm, out_sem)
    store.start()
    heat = FACE_GAIN * pick(onehot, flux, (((0,), (0,)), ((), ())))[:CX]
    heat_ref[...] = heat
    is_even = lax.rem(lax.axis_index("span"), 2) == 0
    even_ref[...] = jnp.where(is_even, heat[CX - 8 :], heat[:8])
    odd_ref[...] = jnp.where(is_even, heat[:8], heat[CX - 8 :])
    store.wait()


def heat_edges_kernel(
    heat_ref, even_in, odd_in, even_packed, odd_packed, rows_ref, even_ref, odd_ref
):
    span_even = lax.rem(lax.axis_index("span"), 2) == 0
    depth_even = lax.rem(lax.axis_index("depth"), 2) == 0
    below = jnp.where(span_even, even_in[...], odd_in[...])
    above = jnp.where(span_even, odd_in[...], even_in[...])
    sub = iota((8, SB), 0)
    rim = jnp.where(sub < 2, below, jnp.where(sub >= 6, above, 0.0))
    rows = jnp.concatenate([heat_ref[...], rim], axis=0)
    rows_ref[...] = rows
    here = lax.shift_right_logical(iota((EX, 128), 1), 1) == DZ
    left = pltpu.roll(rows[:, :128], 2 * DZ, 1)
    right = pltpu.roll(rows[:, 128:], 2 * DZ + 2, 1)
    for packed, out, one, other in (
        (even_packed, even_ref, right, left),
        (odd_packed, odd_ref, left, right),
    ):
        edge = jnp.where(depth_even, one, other)
        out[:EX, :128] = jnp.where(here, edge, packed[:EX, :128])
        out[:EX, 128:] = packed[:EX, 128:]
        out[EX:, :] = packed[EX:, :]


def shell_kernel(
    routes_ref, temp_ref, even_in, odd_in, flux_hbm, out_ref, flux_ref, sems
):
    some = SPAN // CHUNKS
    loads = [
        pltpu.make_async_copy(
            flux_hbm.at[pl.ds(n * some, some)], flux_ref.at[pl.ds(n * some, some)], sems.at[n]
        )
        for n in range(CHUNKS)
    ]
    for load in loads:
        load.start()
    depth_even = lax.rem(lax.axis_index("depth"), 2) == 0
    below = jnp.where(depth_even, even_in[EX : EX + 1, :], odd_in[EX : EX + 1, :])
    above = jnp.where(depth_even, odd_in[EX : EX + 1, :], even_in[EX : EX + 1, :])
    temp = temp_ref[...]
    sub, lane = iota((NB, SB), 0), iota((NB, SB), 1)
    upper = jnp.where(sub == 0, above, pltpu.roll(temp, 1, 0))
    lower = jnp.where(sub == NB - 1, below, pltpu.roll(temp, NB - 1, 0))
    before = jnp.where(lane == 0, 0.0, pltpu.roll(temp, 1, 1))
    after = jnp.where(lane == SB - 1, 0.0, pltpu.roll(temp, SB - 1, 1))
    laplace = lower + upper + after + before - 4.0 * temp
    out_ref[...] = temp + SHELL_RATE * laplace
    target = routes_ref[...].astype(F32)
    target_col = as_column(target, sub == lane)
    same = jnp.logical_and(target_col == target, lane < sub)
    rank_col = jnp.sum(jnp.where(same, 1.0, 0.0), axis=1, keepdims=True)
    position = (target_col * CAP + rank_col).astype(jnp.int32)
    slots = SLOTS // CHUNKS
    total = jnp.zeros((NB, SB), F32)
    for n in range(CHUNKS):
        take = jnp.where(iota((NB, slots), 1) + n * slots == position, 1.0, 0.0).astype(BF16)
        loads[n].wait()
        rows = slice(n * some, (n + 1) * some)
        flux = jnp.concatenate(
            [
                flux_ref[rows, c * CAP : (c + 1) * CAP, :].reshape(slots, 128)
                for c in range(2)
            ],
            axis=1,
        )
        total = total + pick(take, flux)
    out_ref[...] -= SHELL_SINK * total


def swap(even, odd, axis):
    size = lax.axis_size(axis)
    pairs = [(i, i ^ 1) for i in range(size)]
    shifted = [(i, ((i + 1) ^ 1) - 1) for i in range(1, size - 1)]
    return lax.ppermute(even, axis, pairs), lax.ppermute(odd, axis, shifted)


def local(shell_temp, contact_gain, die_temp, diffusivity, routes, tile_rows, closed):
    temp, gain = shell_temp[0], contact_gain[0]
    target = routes.reshape(1, NB)
    die, diff = die_temp.reshape(DZ * CX, SB), diffusivity.reshape(DZ * CX, SB)
    rows = jax.ShapeDtypeStruct((3 * DZ, SB), F32)
    even, odd = pl.pallas_call(
        edge_rows_kernel,
        out_shape=(rows, rows),
        grid=(1,),
        in_specs=[
            pl.BlockSpec((DZ, 8, SB), lambda i: (0, 0, 0)),
            pl.BlockSpec((DZ, 8, SB), lambda i: (0, CX // 8 - 1, 0)),
        ]
        * 2,
        out_specs=(VMEM,) * 2,
        compiler_params=params(60),
        name="edge_rows",
    )(die_temp, die_temp, diffusivity, diffusivity)
    sent = pl.pallas_call(
        pack_kernel,
        out_shape=pltpu.HBM((SPAN * PER, 128), F32),
        in_specs=[HBM] * 5,
        out_specs=HBM,
        scratch_shapes=[
            pltpu.VMEM((1, NB), jnp.int32),
            pltpu.VMEM((1, NB), jnp.int32),
            pltpu.VMEM((1, NB), jnp.int32),
            pltpu.VMEM((NB, SB), F32),
            pltpu.VMEM((NB, SB), F32),
            pltpu.VMEM((SPAN * PER, 128), F32),
            pltpu.SemaphoreType.DMA((5,)),
            pltpu.SemaphoreType.DMA((CHUNKS,)),
        ],
        compiler_params=params(60),
        cost_estimate=cost(6 * SLOTS * NB * 2 * SB, 4 * 2**20),
        name="pack",
    )(target, tile_rows, closed, temp, gain)
    got = lax.all_to_all(
        sent.reshape(SPAN * PER, 1, 128), "span", split_axis=0, concat_axis=0, tiled=True
    ).reshape(SPAN * PER, 128)
    even, odd = swap(even, odd, "span")
    columns, rim = pltpu.HBM((EX + 8, SB), F32), pltpu.HBM((DZ * 8, SB), F32)
    even_packed, odd_packed, die_rim, diff_rim, face = pl.pallas_call(
        edge_columns_kernel,
        out_shape=(columns, columns, rim, rim, pltpu.HBM((CX, SB), F32)),
        grid=(1,),
        in_specs=[VMEM] * 5,
        out_specs=(whole(EX + 8, SB),) * 2 + (whole(DZ * 8, SB),) * 2 + (whole(CX, SB),),
        compiler_params=params(16),
        name="edge_columns",
    )(die, diff, even, odd, temp)

    edge = jax.ShapeDtypeStruct((8, SB), F32)
    flux, heat, even, odd = pl.pallas_call(
        owner_kernel,
        out_shape=(
            pltpu.HBM((2 * SLOTS, 128), F32),
            jax.ShapeDtypeStruct((CX, SB), F32),
            edge,
            edge,
        ),
        grid=(1,),
        in_specs=[HBM, whole(CX, SB)],
        out_specs=(HBM, VMEM, VMEM, VMEM),
        scratch_shapes=[
            pltpu.VMEM((SPAN * PER, 128), F32),
            pltpu.VMEM((2 * SLOTS, 128), F32),
            pltpu.SemaphoreType.DMA((CHUNKS,)),
            pltpu.SemaphoreType.DMA,
        ],
        compiler_params=params(16),
        name="owner",
    )(got, face)
    back = lax.all_to_all(
        flux.reshape(SPAN, 2 * CAP, 128), "span", split_axis=0, concat_axis=0, tiled=True
    )
    even, odd = swap(even, odd, "span")
    heat_rows, even, odd = pl.pallas_call(
        heat_edges_kernel,
        out_shape=(jax.ShapeDtypeStruct((EX, SB), F32),)
        + (jax.ShapeDtypeStruct((EX + 8, SB), F32),) * 2,
        in_specs=[VMEM] * 5,
        out_specs=(VMEM,) * 3,
        compiler_params=params(8),
        cost_estimate=cost(10**12, 2**32),
        name="heat_edges",
    )(heat, even, odd, even_packed, odd_packed)
    even, odd = swap(even, odd, "depth")
    die_next = pl.pallas_call(
        sweeps_kernel,
        out_shape=pltpu.HBM((DZ, CX, SB), F32),
        grid=(1,),
        in_specs=[HBM, HBM, whole(DZ * 8, SB), whole(DZ * 8, SB)] + [VMEM] * 3,
        out_specs=HBM,
        scratch_shapes=[
            pltpu.VMEM((DZ * CX, SB), F32),
            pltpu.VMEM((DZ * CX, SB), F32),
            pltpu.VMEM((DZ, CX, SB), F32),
            pltpu.VMEM((DZ + 2, EX, EY), F32),
            pltpu.VMEM((DZ + 2, EX, EY), F32),
            pltpu.VMEM((DZ, EX, EY), F32),
            pltpu.SemaphoreType.DMA((2 * CHUNKS,)),
            pltpu.SemaphoreType.DMA((CHUNKS,)),
        ],
        compiler_params=params(24),
        name="sweeps",
    )(die, diff, die_rim, diff_rim, heat_rows, even, odd)
    shell_next = pl.pallas_call(
        shell_kernel,
        out_shape=pltpu.HBM((NB, SB), F32),
        grid=(1,),
        in_specs=[VMEM, VMEM, VMEM, VMEM, HBM],
        out_specs=whole(NB, SB),
        scratch_shapes=[
            pltpu.VMEM((SPAN, 2 * CAP, 128), F32),
            pltpu.SemaphoreType.DMA((CHUNKS,)),
        ],
        compiler_params=params(16),
        name="shell",
    )(target, temp, even, odd, back)
    return shell_next[None], die_next


def solution(mesh):
    placed = (
        P("span", "depth", None),
        P("span", "depth", None),
        P(None, "span", "depth"),
        P(None, "span", "depth"),
        P("span", "depth", None),
        P("span", "depth"),
        P("span", "depth"),
    )
    return jax.shard_map(
        local,
        mesh=mesh,
        in_specs=placed,
        out_specs=(P("span", "depth", None), P(None, "span", "depth")),
        check_vma=False,
    )
```

```python
import jax
import jax.numpy as jnp
from jax import lax
from jax.experimental import pallas as pl
from jax.experimental.pallas import tpu as pltpu
from jax.sharding import PartitionSpec as P

SHELL_RATE = 0.15
SHELL_SINK = 0.5
FACE_GAIN = 0.5
F32 = jnp.float32
BF16 = jnp.bfloat16

NB = 256
SB = 256
CX = 32
DZ = 48
CAP = 8
SPAN = 64
SLOTS = SPAN * CAP
PER = 4 * CAP + 1
EX = CX + 8
EY = SB + 128

CHUNKS = 4
UNROLL = 3
GROUP = 4

VMEM = pl.BlockSpec(memory_space=pltpu.VMEM)
HBM = pl.BlockSpec(memory_space=pltpu.HBM)
ANY = pl.BlockSpec(memory_space=pl.ANY)


def whole(*shape):
    return pl.BlockSpec(shape, lambda i: (0,) * len(shape))


def params(mib):
    return pltpu.CompilerParams(vmem_limit_bytes=mib * 2**20)


def cost(flops, moved):
    return pl.CostEstimate(flops=flops, bytes_accessed=moved, transcendentals=0)


def split(x):
    high = x.astype(BF16)
    return high, (x - high.astype(F32)).astype(BF16)


def pick(onehot, x, dims=(((1,), (0,)), ((), ()))):
    total = None
    for part in split(x):
        term = lax.dot_general(onehot, part, dims, preferred_element_type=F32)
        total = term if total is None else total + term
    return total


def iota(shape, dim):
    return lax.broadcasted_iota(jnp.int32, shape, dim)


def as_column(row, eye):
    return jnp.sum(jnp.where(eye, row, 0.0), axis=1, keepdims=True)


def pack_kernel(
    routes_hbm, tile_hbm, closed_hbm, temp_hbm, gain_hbm, out_hbm,
    routes_ref, tile_ref, closed_ref, temp_ref, gain_ref, out_ref, sems, out_sems,
):
    loads = [
        pltpu.make_async_copy(source, target, sems.at[n])
        for n, (source, target) in enumerate(
            (
                (routes_hbm, routes_ref),
                (tile_hbm, tile_ref),
                (closed_hbm, closed_ref),
                (temp_hbm, temp_ref),
                (gain_hbm, gain_ref),
            )
        )
    ]
    for load in loads:
        load.start()
    sub, lane = iota((NB, NB), 0), iota((NB, NB), 1)
    eye = sub == lane
    for load in loads[:3]:
        load.wait()
    target = routes_ref[...].astype(F32)
    same = as_column(target, eye) == target
    rank_row = jnp.sum(
        jnp.where(jnp.logical_and(same, sub < lane), 1.0, 0.0), axis=0, keepdims=True
    )
    rank_col = jnp.sum(
        jnp.where(jnp.logical_and(same, lane < sub), 1.0, 0.0), axis=1, keepdims=True
    )
    tile_col = as_column(tile_ref[...].astype(F32), eye)
    closed_col = as_column(closed_ref[...].astype(F32), eye)
    position = (target * CAP + rank_row).astype(jnp.int32)
    codes = lax.dot_general(
        jnp.where(iota((SPAN, NB), 0) == routes_ref[...], 1.0, 0.0).astype(BF16),
        jnp.where(iota((NB, 128), 1) == rank_col.astype(jnp.int32), tile_col, 0.0).astype(BF16),
        (((1,), (0,)), ((), ())),
        preferred_element_type=F32,
    )
    out_ref[pl.ds(4 * CAP, SPAN, stride=PER), :] = codes
    for load in loads[3:]:
        load.wait()
    parts = split(jnp.concatenate([temp_ref[...], gain_ref[...] * closed_col], axis=1))
    chunk = SPAN // CHUNKS
    stores = []
    for g in range(CHUNKS):
        first = g * chunk * CAP
        put = jnp.where(iota((chunk * CAP, NB), 0) + first == position, 1.0, 0.0).astype(BF16)
        slots = sum(jnp.dot(put, part, preferred_element_type=F32) for part in parts)
        for c in range(4):
            for t in range(chunk):
                out_ref[pl.ds((g * chunk + t) * PER + c, CAP, stride=4), :] = slots[
                    t * CAP : (t + 1) * CAP, c * 128 : (c + 1) * 128
                ]
        rows = pl.ds(g * chunk * PER, chunk * PER)
        stores.append(pltpu.make_async_copy(out_ref.at[rows], out_hbm.at[rows], out_sems.at[g]))
        stores[-1].start()
    for store in stores:
        store.wait()


def edge_rows_kernel(die_first, die_last, diff_first, diff_last, even_ref, odd_ref):
    is_even = lax.rem(lax.axis_index("span"), 2) == 0

    def layer(z, carry):
        for n, (first, low, last, high) in enumerate(
            ((die_first, 0, die_last, 6), (die_first, 1, die_last, 7), (diff_first, 0, diff_last, 7))
        ):
            top = first[z, low : low + 1, :]
            bottom = last[z, high : high + 1, :]
            even_ref[pl.ds(n * DZ + z, 1), :] = jnp.where(is_even, bottom, top)
            odd_ref[pl.ds(n * DZ + z, 1), :] = jnp.where(is_even, top, bottom)
        return carry

    lax.fori_loop(0, DZ, layer, 0, unroll=8)


def edge_columns_kernel(
    die_ref, diff_ref, even_in, odd_in, temp_ref, even_ref, odd_ref, die_rim, diff_rim, face_ref
):
    span_even = lax.rem(lax.axis_index("span"), 2) == 0
    depth_even = lax.rem(lax.axis_index("depth"), 2) == 0
    sub = iota((8, SB), 0)

    def rim_of(z, spots):
        tile = jnp.zeros((8, SB), F32)
        for spot, n, up in spots:
            at = pl.ds(n * DZ + z, 1)
            row = jnp.where(span_even != up, even_in[at, :], odd_in[at, :])
            tile = jnp.where(sub == spot, row, tile)
        return tile

    lane = iota((EX, 128), 1)

    def add_layer(z, kept):
        v_left, v_right, k_left, k_right = kept
        rows, rim = pl.ds(pl.multiple_of(z * CX, CX), CX), pl.ds(pl.multiple_of(z * 8, 8), 8)
        v_rim = rim_of(z, ((0, 0, False), (1, 1, False), (6, 0, True), (7, 1, True)))
        k_rim = rim_of(z, ((0, 2, False), (7, 2, True)))
        die_rim[rim, :] = v_rim
        diff_rim[rim, :] = k_rim
        v = jnp.concatenate([die_ref[rows, :], v_rim], axis=0)
        k = jnp.concatenate([diff_ref[rows, :], k_rim], axis=0)
        here = lax.shift_right_logical(lane, 1) == z
        v_left = jnp.where(here, pltpu.roll(v[:, :128], 2 * z, 1), v_left)
        v_right = jnp.where(here, pltpu.roll(v[:, 128:], 2 * z + 2, 1), v_right)
        k_left = jnp.where(here, pltpu.roll(k[:, :128], 2 * z, 1), k_left)
        k_right = jnp.where(here, pltpu.roll(k[:, 128:], 2 * z + 2, 1), k_right)
        return v_left, v_right, k_left, k_right

    none = jnp.zeros((EX, 128), F32)
    v_left, v_right, k_left, k_right = lax.fori_loop(0, DZ, add_layer, (none,) * 4, unroll=8)
    even_ref[:EX, :128] = jnp.where(depth_even, v_right, v_left)
    even_ref[:EX, 128:] = jnp.where(depth_even, k_right, k_left)
    odd_ref[:EX, :128] = jnp.where(depth_even, v_left, v_right)
    odd_ref[:EX, 128:] = jnp.where(depth_even, k_left, k_right)
    first, last = temp_ref[0:1, :], temp_ref[NB - 1 : NB, :]
    even_ref[EX:, :] = jnp.broadcast_to(jnp.where(depth_even, last, first), (8, SB))
    odd_ref[EX:, :] = jnp.broadcast_to(jnp.where(depth_even, first, last), (8, SB))
    face_ref[...] = die_ref[:CX, :]


def across(p):
    q = p + 0.5 * (pltpu.roll(p, 1, 1) + pltpu.roll(p, p.shape[1] - 1, 1))
    return q + 0.5 * (pltpu.roll(q, 1, 0) + pltpu.roll(q, q.shape[0] - 1, 0))


def sweeps_kernel(
    die_hbm, diff_hbm, die_rim, diff_rim, after_ref, out_ref,
    die_ref, diff_ref, field, later, rate, sems,
):
    del after_ref
    some = DZ // CHUNKS
    loads = []
    for n in range(CHUNKS):
        for m, (source, target) in enumerate(((die_hbm, die_ref), (diff_hbm, diff_ref))):
            rows = pl.ds(n * some * CX, some * CX)
            loads.append(
                pltpu.make_async_copy(source.at[rows], target.at[rows], sems.at[2 * n + m])
            )
            loads[-1].start()
    none = jnp.zeros((EX, SB), F32)
    for ref in (field, later):
        ref[0] = none
        ref[DZ + 1] = none
    for n in range(CHUNKS):
        loads[2 * n].wait()
        loads[2 * n + 1].wait()
        for z in range(n * some, (n + 1) * some):
            field[z + 1, :CX] = die_ref[z * CX : (z + 1) * CX, :]
            field[z + 1, CX:] = die_rim[z * 8 : (z + 1) * 8, :]
            rate[z, :CX] = diff_ref[z * CX : (z + 1) * CX, :]
            rate[z, CX:] = diff_rim[z * 8 : (z + 1) * 8, :]
    gap = jnp.abs(iota((SB, SB), 0) - iota((SB, SB), 1))
    band = jnp.where(gap == 0, 1.0, jnp.where(gap == 1, 0.5, 0.0)).astype(BF16)

    def around(ref, start):
        layers = []
        for n in range(GROUP):
            z = start + n
            layers.append(2.0 * ref[z + 1] + (ref[z] + ref[z + 2]))
        p = jnp.concatenate(layers, axis=0)
        high, low = split(p)
        q = jnp.dot(high, band, preferred_element_type=F32)
        q = q + jnp.dot(low, band, preferred_element_type=F32)
        for n in range(GROUP):
            own = q[n * EX : (n + 1) * EX]
            yield own + 0.5 * (pltpu.roll(own, 1, 0) + pltpu.roll(own, EX - 1, 0))

    def first(g, carry):
        for n, q in enumerate(around(field, g * GROUP)):
            z = g * GROUP + n
            v = field[z + 1]
            later[z + 1] = v + rate[z] * (q - 16.0 * v)
        return carry

    lax.fori_loop(0, DZ // GROUP, first, 0, unroll=4 * UNROLL)

    def second(g, carry):
        for n, q in enumerate(around(later, g * GROUP)):
            z = g * GROUP + n
            v = later[z + 1, :CX]
            out_ref[z] = v + rate[z, :CX] * (q[:CX] - 16.0 * v)
        return carry

    lax.fori_loop(0, DZ // GROUP, second, 0, unroll=4 * UNROLL)


def smooth(x):
    z = 2.0 * x + (pltpu.roll(x, 2, 1) + pltpu.roll(x, 126, 1))
    return z + 0.5 * (pltpu.roll(z, 1, 0) + pltpu.roll(z, EX - 1, 0))


def finish_kernel(
    base_ref, diff_top, diff_rim, heat_ref, even_own, odd_own, even_in, odd_in, out_hbm,
    out_ref, out_sems,
):
    some = DZ // CHUNKS
    depth_even = lax.rem(lax.axis_index("depth"), 2) == 0
    lane = iota((EX, 128), 1)
    die = lane < 2 * DZ
    first_lane = jnp.logical_and(die, lax.rem(lane, 2) == 0)
    second_lane = jnp.logical_and(die, lax.rem(lane, 2) == 1)

    def parts(even_ref, odd_ref, when):
        v = jnp.where(when, even_ref[:EX, :128], odd_ref[:EX, :128])
        return v, jnp.where(when, even_ref[:EX, 128:], odd_ref[:EX, 128:])

    right_v, right_k = parts(even_own, odd_own, depth_even)
    left_v, left_k = parts(even_own, odd_own, jnp.logical_not(depth_even))
    after_v, after_k = parts(even_in, odd_in, depth_even)
    before_v, before_k = parts(even_in, odd_in, jnp.logical_not(depth_even))

    def up(x):
        return pltpu.roll(x, 1, 1)

    def down(x):
        return pltpu.roll(x, 127, 1)

    def change(own_v, own_k, out_v, out_k, outer, inner, to_outer, to_inner):
        own_w, out_w = smooth(jnp.where(die, own_v, 0.0)), smooth(jnp.where(die, out_v, 0.0))
        near = out_v + out_k * (
            out_w + 0.5 * (to_outer(out_w) + to_outer(own_w)) - 16.0 * out_v
        )
        near = jnp.where(outer, near, 0.0)
        moved = jnp.where(inner, 0.5 * own_k * to_inner(out_w), 0.0)
        spread = smooth(moved)
        edge = moved + own_k * (spread - 16.0 * moved + 0.5 * to_inner(smooth(near)))
        return jnp.where(inner, edge, jnp.where(die, 0.5 * own_k * to_outer(spread), 0.0))

    left = change(left_v, left_k, before_v, before_k, second_lane, first_lane, up, down)
    right = change(right_v, right_k, after_v, after_k, first_lane, second_lane, down, up)

    h_right, h_left = pltpu.roll(after_v, 128 - 2 * DZ, 1), pltpu.roll(before_v, 126 - 2 * DZ, 1)
    rim = jnp.where(lane < 2, h_right, jnp.where(lane >= 126, h_left, 0.0))
    heat = jnp.concatenate([heat_ref[...], rim], axis=1)
    rates = []
    for z in range(3):
        k_right = pltpu.roll(after_k, (128 - 2 * z) % 128, 1)
        k_left = pltpu.roll(before_k, 126 - 2 * z, 1)
        k_rim = jnp.where(lane < 1, k_right, jnp.where(lane >= 127, k_left, 0.0))
        own = jnp.concatenate([diff_top[z], diff_rim[z * 8 : (z + 1) * 8, :]], axis=0)
        rates.append(jnp.concatenate([own, k_rim], axis=1))
    around = across(heat)
    first = heat + rates[0] * (2.0 * around - 16.0 * heat)
    second = rates[1] * around
    added = []
    for rate, own, p in (
        (rates[0], first, 2.0 * first + second),
        (rates[1], second, 2.0 * second + first),
        (rates[2], 0.0, second),
    ):
        added.append((own + rate * (across(p) - 16.0 * own))[:CX, :SB])

    left, right = left[:CX], right[:CX]
    edge = iota((CX, 128), 1)
    stores = []
    for n in range(CHUNKS):
        for z in range(n * some, (n + 1) * some):
            at_left = pltpu.roll(left, (128 - 2 * z) % 128, 1)
            at_right = pltpu.roll(right, 126 - 2 * z, 1)
            near = jnp.where(edge < 2, at_left, 0.0)
            far = jnp.where(edge >= 126, at_right, 0.0)
            step = jnp.concatenate([near, far], axis=1)
            if z < 3:
                step = step + added[z]
            out_ref[z] = base_ref[z] + step
        layers = pl.ds(n * some, some)
        stores.append(
            pltpu.make_async_copy(out_ref.at[layers], out_hbm.at[layers], out_sems.at[n])
        )
        stores[-1].start()
    for store in stores:
        store.wait()


def owner_kernel(
    got_hbm, face_ref, flux_hbm, heat_ref, even_ref, odd_ref,
    got_ref, flux_ref, sems, out_sem,
):
    rows = SPAN * PER // CHUNKS
    loads = [
        pltpu.make_async_copy(
            got_hbm.at[pl.ds(n * rows, rows)], got_ref.at[pl.ds(n * rows, rows)], sems.at[n]
        )
        for n in range(CHUNKS)
    ]
    for load in loads:
        load.start()
    lane = iota((SPAN, 128), 1).astype(F32)
    faces = jnp.concatenate([face_ref[...], jnp.zeros((128 - CX, SB), F32)], axis=0)
    for load in loads:
        load.wait()
    codes = got_ref[pl.ds(4 * CAP, SPAN, stride=PER), :]
    onehot = jnp.concatenate(
        [jnp.where(codes[:, k : k + 1] == lane, 1.0, 0.0) for k in range(CAP)], axis=0
    ).astype(BF16)
    touched = pick(onehot, faces)

    def slots(c):
        return jnp.concatenate(
            [got_ref[pl.ds(k * 4 + c, SPAN, stride=PER), :] for k in range(CAP)], axis=0
        )

    temp = jnp.concatenate([slots(0), slots(1)], axis=1)
    gain = jnp.concatenate([slots(2), slots(3)], axis=1)
    flux = gain * (temp - touched)
    for k in range(CAP):
        for c in range(2):
            flux_ref[pl.ds(c * CAP + k, SPAN, stride=2 * CAP), :] = flux[
                k * SPAN : (k + 1) * SPAN, c * 128 : (c + 1) * 128
            ]
    store = pltpu.make_async_copy(flux_ref, flux_hbm, out_sem)
    store.start()
    heat = FACE_GAIN * pick(onehot, flux, (((0,), (0,)), ((), ())))[:CX]
    heat_ref[...] = heat
    is_even = lax.rem(lax.axis_index("span"), 2) == 0
    even_ref[...] = jnp.where(is_even, heat[CX - 8 :], heat[:8])
    odd_ref[...] = jnp.where(is_even, heat[:8], heat[CX - 8 :])
    store.wait()


def heat_edges_kernel(
    heat_ref, even_in, odd_in, even_packed, odd_packed, rows_ref, even_ref, odd_ref
):
    span_even = lax.rem(lax.axis_index("span"), 2) == 0
    depth_even = lax.rem(lax.axis_index("depth"), 2) == 0
    below = jnp.where(span_even, even_in[...], odd_in[...])
    above = jnp.where(span_even, odd_in[...], even_in[...])
    sub = iota((8, SB), 0)
    rim = jnp.where(sub < 2, below, jnp.where(sub >= 6, above, 0.0))
    rows = jnp.concatenate([heat_ref[...], rim], axis=0)
    rows_ref[...] = rows
    here = lax.shift_right_logical(iota((EX, 128), 1), 1) == DZ
    left = pltpu.roll(rows[:, :128], 2 * DZ, 1)
    right = pltpu.roll(rows[:, 128:], 2 * DZ + 2, 1)
    for packed, out, one, other in (
        (even_packed, even_ref, right, left),
        (odd_packed, odd_ref, left, right),
    ):
        edge = jnp.where(depth_even, one, other)
        out[:EX, :128] = jnp.where(here, edge, packed[:EX, :128])
        out[:EX, 128:] = packed[:EX, 128:]
        out[EX:, :] = packed[EX:, :]


def shell_kernel(
    routes_ref, temp_ref, even_in, odd_in, flux_hbm, out_ref, flux_ref, sems
):
    some = SPAN // CHUNKS
    loads = [
        pltpu.make_async_copy(
            flux_hbm.at[pl.ds(n * some, some)], flux_ref.at[pl.ds(n * some, some)], sems.at[n]
        )
        for n in range(CHUNKS)
    ]
    for load in loads:
        load.start()
    depth_even = lax.rem(lax.axis_index("depth"), 2) == 0
    below = jnp.where(depth_even, even_in[EX : EX + 1, :], odd_in[EX : EX + 1, :])
    above = jnp.where(depth_even, odd_in[EX : EX + 1, :], even_in[EX : EX + 1, :])
    temp = temp_ref[...]
    sub, lane = iota((NB, SB), 0), iota((NB, SB), 1)
    upper = jnp.where(sub == 0, above, pltpu.roll(temp, 1, 0))
    lower = jnp.where(sub == NB - 1, below, pltpu.roll(temp, NB - 1, 0))
    before = jnp.where(lane == 0, 0.0, pltpu.roll(temp, 1, 1))
    after = jnp.where(lane == SB - 1, 0.0, pltpu.roll(temp, SB - 1, 1))
    laplace = lower + upper + after + before - 4.0 * temp
    out_ref[...] = temp + SHELL_RATE * laplace
    target = routes_ref[...].astype(F32)
    target_col = as_column(target, sub == lane)
    same = jnp.logical_and(target_col == target, lane < sub)
    rank_col = jnp.sum(jnp.where(same, 1.0, 0.0), axis=1, keepdims=True)
    position = (target_col * CAP + rank_col).astype(jnp.int32)
    slots = SLOTS // CHUNKS
    total = jnp.zeros((NB, SB), F32)
    for n in range(CHUNKS):
        take = jnp.where(iota((NB, slots), 1) + n * slots == position, 1.0, 0.0).astype(BF16)
        loads[n].wait()
        rows = slice(n * some, (n + 1) * some)
        flux = jnp.concatenate(
            [
                flux_ref[rows, c * CAP : (c + 1) * CAP, :].reshape(slots, 128)
                for c in range(2)
            ],
            axis=1,
        )
        total = total + pick(take, flux)
    out_ref[...] -= SHELL_SINK * total


def swap(even, odd, axis):
    size = lax.axis_size(axis)
    pairs = [(i, i ^ 1) for i in range(size)]
    shifted = [(i, ((i + 1) ^ 1) - 1) for i in range(1, size - 1)]
    return lax.ppermute(even, axis, pairs), lax.ppermute(odd, axis, shifted)


def local(shell_temp, contact_gain, die_temp, diffusivity, routes, tile_rows, closed):
    temp, gain = shell_temp[0], contact_gain[0]
    target = routes.reshape(1, NB)
    die, diff = die_temp.reshape(DZ * CX, SB), diffusivity.reshape(DZ * CX, SB)
    rows = jax.ShapeDtypeStruct((3 * DZ, SB), F32)
    even, odd = pl.pallas_call(
        edge_rows_kernel,
        out_shape=(rows, rows),
        grid=(1,),
        in_specs=[
            pl.BlockSpec((DZ, 8, SB), lambda i: (0, 0, 0)),
            pl.BlockSpec((DZ, 8, SB), lambda i: (0, CX // 8 - 1, 0)),
        ]
        * 2,
        out_specs=(VMEM,) * 2,
        compiler_params=params(60),
        name="edge_rows",
    )(die_temp, die_temp, diffusivity, diffusivity)
    sent = pl.pallas_call(
        pack_kernel,
        out_shape=pltpu.HBM((SPAN * PER, 128), F32),
        in_specs=[HBM] * 5,
        out_specs=HBM,
        scratch_shapes=[
            pltpu.VMEM((1, NB), jnp.int32),
            pltpu.VMEM((1, NB), jnp.int32),
            pltpu.VMEM((1, NB), jnp.int32),
            pltpu.VMEM((NB, SB), F32),
            pltpu.VMEM((NB, SB), F32),
            pltpu.VMEM((SPAN * PER, 128), F32),
            pltpu.SemaphoreType.DMA((5,)),
            pltpu.SemaphoreType.DMA((CHUNKS,)),
        ],
        compiler_params=params(60),
        cost_estimate=cost(6 * SLOTS * NB * 2 * SB, 4 * 2**20),
        name="pack",
    )(target, tile_rows, closed, temp, gain)
    got = lax.all_to_all(
        sent.reshape(SPAN * PER, 1, 128), "span", split_axis=0, concat_axis=0, tiled=True
    ).reshape(SPAN * PER, 128)
    even, odd = swap(even, odd, "span")
    columns, rim = pltpu.HBM((EX + 8, SB), F32), pltpu.HBM((DZ * 8, SB), F32)
    even_packed, odd_packed, die_rim, diff_rim, face = pl.pallas_call(
        edge_columns_kernel,
        out_shape=(columns, columns, rim, rim, pltpu.HBM((CX, SB), F32)),
        grid=(1,),
        in_specs=[VMEM] * 5,
        out_specs=(whole(EX + 8, SB),) * 2 + (whole(DZ * 8, SB),) * 2 + (whole(CX, SB),),
        compiler_params=params(16),
        name="edge_columns",
    )(die, diff, even, odd, temp)

    edge = jax.ShapeDtypeStruct((8, SB), F32)
    flux, heat, even, odd = pl.pallas_call(
        owner_kernel,
        out_shape=(
            pltpu.HBM((2 * SLOTS, 128), F32),
            jax.ShapeDtypeStruct((CX, SB), F32),
            edge,
            edge,
        ),
        grid=(1,),
        in_specs=[HBM, whole(CX, SB)],
        out_specs=(HBM, VMEM, VMEM, VMEM),
        scratch_shapes=[
            pltpu.VMEM((SPAN * PER, 128), F32),
            pltpu.VMEM((2 * SLOTS, 128), F32),
            pltpu.SemaphoreType.DMA((CHUNKS,)),
            pltpu.SemaphoreType.DMA,
        ],
        compiler_params=params(16),
        name="owner",
    )(got, face)
    back = lax.all_to_all(
        flux.reshape(SPAN, 2 * CAP, 128), "span", split_axis=0, concat_axis=0, tiled=True
    )
    even, odd = swap(even, odd, "span")
    heat_rows, even, odd = pl.pallas_call(
        heat_edges_kernel,
        out_shape=(jax.ShapeDtypeStruct((EX, SB), F32),)
        + (jax.ShapeDtypeStruct((EX + 8, SB), F32),) * 2,
        in_specs=[VMEM] * 5,
        out_specs=(VMEM,) * 3,
        compiler_params=params(8),
        cost_estimate=cost(10**12, 2**32),
        name="heat_edges",
    )(heat, even, odd, even_packed, odd_packed)
    base = pl.pallas_call(
        sweeps_kernel,
        out_shape=jax.ShapeDtypeStruct((DZ, CX, SB), F32),
        grid=(1,),
        in_specs=[HBM, HBM, whole(DZ * 8, SB), whole(DZ * 8, SB), VMEM],
        out_specs=VMEM,
        scratch_shapes=[
            pltpu.VMEM((DZ * CX, SB), F32),
            pltpu.VMEM((DZ * CX, SB), F32),
            pltpu.VMEM((DZ + 2, EX, SB), F32),
            pltpu.VMEM((DZ + 2, EX, SB), F32),
            pltpu.VMEM((DZ, EX, SB), F32),
            pltpu.SemaphoreType.DMA((2 * CHUNKS,)),
        ],
        compiler_params=params(24),
        name="sweeps",
    )(die, diff, die_rim, diff_rim, heat_rows)
    even_own, odd_own = even, odd
    even, odd = swap(even, odd, "depth")
    die_next = pl.pallas_call(
        finish_kernel,
        out_shape=pltpu.HBM((DZ, CX, SB), F32),
        grid=(1,),
        in_specs=[
            VMEM,
            whole(3, CX, SB),
            pl.BlockSpec((24, SB), lambda i: (0, 0)),
        ]
        + [VMEM] * 5,
        out_specs=HBM,
        scratch_shapes=[
            pltpu.VMEM((DZ, CX, SB), F32),
            pltpu.SemaphoreType.DMA((CHUNKS,)),
        ],
        compiler_params=params(16),
        name="finish",
    )(base, diffusivity, diff_rim, heat_rows, even_own, odd_own, even, odd)
    shell_next = pl.pallas_call(
        shell_kernel,
        out_shape=pltpu.HBM((NB, SB), F32),
        grid=(1,),
        in_specs=[VMEM, VMEM, VMEM, VMEM, HBM],
        out_specs=whole(NB, SB),
        scratch_shapes=[
            pltpu.VMEM((SPAN, 2 * CAP, 128), F32),
            pltpu.SemaphoreType.DMA((CHUNKS,)),
        ],
        compiler_params=params(16),
        name="shell",
    )(target, temp, even, odd, back)
    return shell_next[None], die_next


def solution(mesh):
    placed = (
        P("span", "depth", None),
        P("span", "depth", None),
        P(None, "span", "depth"),
        P(None, "span", "depth"),
        P("span", "depth", None),
        P("span", "depth"),
        P("span", "depth"),
    )
    return jax.shard_map(
        local,
        mesh=mesh,
        in_specs=placed,
        out_specs=(P("span", "depth", None), P(None, "span", "depth")),
        check_vma=False,
    )
```

```python
import jax
import jax.numpy as jnp
from jax import lax
from jax.experimental import pallas as pl
from jax.experimental.pallas import tpu as pltpu
from jax.sharding import PartitionSpec as P

SHELL_RATE = 0.15
SHELL_SINK = 0.5
FACE_GAIN = 0.5
F32 = jnp.float32
BF16 = jnp.bfloat16

NB = 256
SB = 256
CX = 32
DZ = 48
CAP = 8
SPAN = 64
SLOTS = SPAN * CAP
PER = 4 * CAP + 1
EX = CX + 8
EY = SB + 128

CHUNKS = 4
UNROLL = 3
GROUP = 4

VMEM = pl.BlockSpec(memory_space=pltpu.VMEM)
HBM = pl.BlockSpec(memory_space=pltpu.HBM)
ANY = pl.BlockSpec(memory_space=pl.ANY)


def whole(*shape):
    return pl.BlockSpec(shape, lambda i: (0,) * len(shape))


def params(mib):
    return pltpu.CompilerParams(vmem_limit_bytes=mib * 2**20)


def cost(flops, moved):
    return pl.CostEstimate(flops=flops, bytes_accessed=moved, transcendentals=0)


def split(x):
    high = x.astype(BF16)
    return high, (x - high.astype(F32)).astype(BF16)


def pick(onehot, x, dims=(((1,), (0,)), ((), ()))):
    total = None
    for part in split(x):
        term = lax.dot_general(onehot, part, dims, preferred_element_type=F32)
        total = term if total is None else total + term
    return total


def iota(shape, dim):
    return lax.broadcasted_iota(jnp.int32, shape, dim)


def as_column(row, eye):
    return jnp.sum(jnp.where(eye, row, 0.0), axis=1, keepdims=True)


def pack_kernel(
    routes_hbm, tile_hbm, closed_hbm, temp_hbm, gain_hbm, out_hbm,
    routes_ref, tile_ref, closed_ref, temp_ref, gain_ref, out_ref, sems, out_sems,
):
    loads = [
        pltpu.make_async_copy(source, target, sems.at[n])
        for n, (source, target) in enumerate(
            (
                (routes_hbm, routes_ref),
                (tile_hbm, tile_ref),
                (closed_hbm, closed_ref),
                (temp_hbm, temp_ref),
                (gain_hbm, gain_ref),
            )
        )
    ]
    for load in loads:
        load.start()
    sub, lane = iota((NB, NB), 0), iota((NB, NB), 1)
    eye = sub == lane
    for load in loads[:3]:
        load.wait()
    target = routes_ref[...].astype(F32)
    same = as_column(target, eye) == target
    rank_row = jnp.sum(
        jnp.where(jnp.logical_and(same, sub < lane), 1.0, 0.0), axis=0, keepdims=True
    )
    rank_col = jnp.sum(
        jnp.where(jnp.logical_and(same, lane < sub), 1.0, 0.0), axis=1, keepdims=True
    )
    tile_col = as_column(tile_ref[...].astype(F32), eye)
    closed_col = as_column(closed_ref[...].astype(F32), eye)
    position = (target * CAP + rank_row).astype(jnp.int32)
    codes = lax.dot_general(
        jnp.where(iota((SPAN, NB), 0) == routes_ref[...], 1.0, 0.0).astype(BF16),
        jnp.where(iota((NB, 128), 1) == rank_col.astype(jnp.int32), tile_col, 0.0).astype(BF16),
        (((1,), (0,)), ((), ())),
        preferred_element_type=F32,
    )
    out_ref[pl.ds(4 * CAP, SPAN, stride=PER), :] = codes
    for load in loads[3:]:
        load.wait()
    parts = split(jnp.concatenate([temp_ref[...], gain_ref[...] * closed_col], axis=1))
    chunk = SPAN // CHUNKS
    stores = []
    for g in range(CHUNKS):
        first = g * chunk * CAP
        put = jnp.where(iota((chunk * CAP, NB), 0) + first == position, 1.0, 0.0).astype(BF16)
        slots = sum(jnp.dot(put, part, preferred_element_type=F32) for part in parts)
        for c in range(4):
            for t in range(chunk):
                out_ref[pl.ds((g * chunk + t) * PER + c, CAP, stride=4), :] = slots[
                    t * CAP : (t + 1) * CAP, c * 128 : (c + 1) * 128
                ]
        rows = pl.ds(g * chunk * PER, chunk * PER)
        stores.append(pltpu.make_async_copy(out_ref.at[rows], out_hbm.at[rows], out_sems.at[g]))
        stores[-1].start()
    for store in stores:
        store.wait()


def edge_rows_kernel(die_first, die_last, diff_first, diff_last, even_ref, odd_ref):
    is_even = lax.rem(lax.axis_index("span"), 2) == 0

    def layer(z, carry):
        for n, (first, low, last, high) in enumerate(
            ((die_first, 0, die_last, 6), (die_first, 1, die_last, 7), (diff_first, 0, diff_last, 7))
        ):
            top = first[z, low : low + 1, :]
            bottom = last[z, high : high + 1, :]
            even_ref[pl.ds(n * DZ + z, 1), :] = jnp.where(is_even, bottom, top)
            odd_ref[pl.ds(n * DZ + z, 1), :] = jnp.where(is_even, top, bottom)
        return carry

    lax.fori_loop(0, DZ, layer, 0, unroll=8)


def edge_columns_kernel(
    die_ref, diff_ref, even_in, odd_in, temp_ref, even_ref, odd_ref, die_rim, diff_rim, face_ref
):
    span_even = lax.rem(lax.axis_index("span"), 2) == 0
    depth_even = lax.rem(lax.axis_index("depth"), 2) == 0
    sub = iota((8, SB), 0)

    def rim_of(z, spots):
        tile = jnp.zeros((8, SB), F32)
        for spot, n, up in spots:
            at = pl.ds(n * DZ + z, 1)
            row = jnp.where(span_even != up, even_in[at, :], odd_in[at, :])
            tile = jnp.where(sub == spot, row, tile)
        return tile

    lane = iota((EX, 128), 1)

    def add_layer(z, kept):
        v_left, v_right, k_left, k_right = kept
        rows, rim = pl.ds(pl.multiple_of(z * CX, CX), CX), pl.ds(pl.multiple_of(z * 8, 8), 8)
        v_rim = rim_of(z, ((0, 0, False), (1, 1, False), (6, 0, True), (7, 1, True)))
        k_rim = rim_of(z, ((0, 2, False), (7, 2, True)))
        die_rim[rim, :] = v_rim
        diff_rim[rim, :] = k_rim
        v = jnp.concatenate([die_ref[rows, :], v_rim], axis=0)
        k = jnp.concatenate([diff_ref[rows, :], k_rim], axis=0)
        here = lax.shift_right_logical(lane, 1) == z
        v_left = jnp.where(here, pltpu.roll(v[:, :128], 2 * z, 1), v_left)
        v_right = jnp.where(here, pltpu.roll(v[:, 128:], 2 * z + 2, 1), v_right)
        k_left = jnp.where(here, pltpu.roll(k[:, :128], 2 * z, 1), k_left)
        k_right = jnp.where(here, pltpu.roll(k[:, 128:], 2 * z + 2, 1), k_right)
        return v_left, v_right, k_left, k_right

    none = jnp.zeros((EX, 128), F32)
    v_left, v_right, k_left, k_right = lax.fori_loop(0, DZ, add_layer, (none,) * 4, unroll=8)
    even_ref[:EX, :128] = jnp.where(depth_even, v_right, v_left)
    even_ref[:EX, 128:] = jnp.where(depth_even, k_right, k_left)
    odd_ref[:EX, :128] = jnp.where(depth_even, v_left, v_right)
    odd_ref[:EX, 128:] = jnp.where(depth_even, k_left, k_right)
    first, last = temp_ref[0:1, :], temp_ref[NB - 1 : NB, :]
    even_ref[EX:, :] = jnp.broadcast_to(jnp.where(depth_even, last, first), (8, SB))
    odd_ref[EX:, :] = jnp.broadcast_to(jnp.where(depth_even, first, last), (8, SB))
    face_ref[...] = die_ref[:CX, :]


def across(p):
    q = p + 0.5 * (pltpu.roll(p, 1, 1) + pltpu.roll(p, p.shape[1] - 1, 1))
    return q + 0.5 * (pltpu.roll(q, 1, 0) + pltpu.roll(q, q.shape[0] - 1, 0))


def sweeps_kernel(
    die_hbm, diff_hbm, die_rim, diff_rim, after_ref, out_ref,
    die_ref, diff_ref, field, later, rate, sems,
):
    del after_ref
    some = DZ // CHUNKS
    loads = []
    for n in range(CHUNKS):
        for m, (source, target) in enumerate(((die_hbm, die_ref), (diff_hbm, diff_ref))):
            rows = pl.ds(n * some * CX, some * CX)
            loads.append(
                pltpu.make_async_copy(source.at[rows], target.at[rows], sems.at[2 * n + m])
            )
            loads[-1].start()
    none = jnp.zeros((EX, SB), F32)
    for ref in (field, later):
        ref[0] = none
        ref[DZ + 1] = none
    for n in range(CHUNKS):
        loads[2 * n].wait()
        loads[2 * n + 1].wait()
        for z in range(n * some, (n + 1) * some):
            field[z + 1, :CX] = die_ref[z * CX : (z + 1) * CX, :]
            field[z + 1, CX:] = die_rim[z * 8 : (z + 1) * 8, :]
            rate[z, :CX] = diff_ref[z * CX : (z + 1) * CX, :]
            rate[z, CX:] = diff_rim[z * 8 : (z + 1) * 8, :]
    gap = jnp.abs(iota((SB, SB), 0) - iota((SB, SB), 1))
    band = jnp.where(gap == 0, 1.0, jnp.where(gap == 1, 0.5, 0.0)).astype(BF16)

    def around(ref, start):
        layers = []
        for n in range(GROUP):
            z = start + n
            layers.append(2.0 * ref[z + 1] + (ref[z] + ref[z + 2]))
        p = jnp.concatenate(layers, axis=0)
        high, low = split(p)
        q = jnp.dot(high, band, preferred_element_type=F32)
        q = q + jnp.dot(low, band, preferred_element_type=F32)
        for n in range(GROUP):
            own = q[n * EX : (n + 1) * EX]
            yield own + 0.5 * (pltpu.roll(own, 1, 0) + pltpu.roll(own, EX - 1, 0))

    def first(g, carry):
        for n, q in enumerate(around(field, g * GROUP)):
            z = g * GROUP + n
            v = field[z + 1]
            later[z + 1] = v + rate[z] * (q - 16.0 * v)
        return carry

    lax.fori_loop(0, DZ // GROUP, first, 0, unroll=4 * UNROLL)

    def second(g, carry):
        for n, q in enumerate(around(later, g * GROUP)):
            z = g * GROUP + n
            v = later[z + 1, :CX]
            out_ref[z] = v + rate[z, :CX] * (q[:CX] - 16.0 * v)
        return carry

    lax.fori_loop(0, DZ // GROUP, second, 0, unroll=4 * UNROLL)


def smooth(x):
    z = 2.0 * x + (pltpu.roll(x, 2, 1) + pltpu.roll(x, 126, 1))
    return z + 0.5 * (pltpu.roll(z, 1, 0) + pltpu.roll(z, EX - 1, 0))


def finish_kernel(
    base_ref, diff_top, diff_rim, heat_ref, even_own, odd_own, even_in, odd_in, out_hbm,
    out_ref, out_sems,
):
    some = DZ // CHUNKS
    depth_even = lax.rem(lax.axis_index("depth"), 2) == 0
    lane = iota((EX, 128), 1)
    die = lane < 2 * DZ
    first_lane = jnp.logical_and(die, lax.rem(lane, 2) == 0)
    second_lane = jnp.logical_and(die, lax.rem(lane, 2) == 1)

    def parts(even_ref, odd_ref, when):
        v = jnp.where(when, even_ref[:EX, :128], odd_ref[:EX, :128])
        return v, jnp.where(when, even_ref[:EX, 128:], odd_ref[:EX, 128:])

    right_v, right_k = parts(even_own, odd_own, depth_even)
    left_v, left_k = parts(even_own, odd_own, jnp.logical_not(depth_even))
    after_v, after_k = parts(even_in, odd_in, depth_even)
    before_v, before_k = parts(even_in, odd_in, jnp.logical_not(depth_even))

    def up(x):
        return pltpu.roll(x, 1, 1)

    def down(x):
        return pltpu.roll(x, 127, 1)

    def change(own_v, own_k, out_v, out_k, outer, inner, to_outer, to_inner):
        own_w, out_w = smooth(jnp.where(die, own_v, 0.0)), smooth(jnp.where(die, out_v, 0.0))
        near = out_v + out_k * (
            out_w + 0.5 * (to_outer(out_w) + to_outer(own_w)) - 16.0 * out_v
        )
        near = jnp.where(outer, near, 0.0)
        moved = jnp.where(inner, 0.5 * own_k * to_inner(out_w), 0.0)
        spread = smooth(moved)
        edge = moved + own_k * (spread - 16.0 * moved + 0.5 * to_inner(smooth(near)))
        return jnp.where(inner, edge, jnp.where(die, 0.5 * own_k * to_outer(spread), 0.0))

    left = change(left_v, left_k, before_v, before_k, second_lane, first_lane, up, down)
    right = change(right_v, right_k, after_v, after_k, first_lane, second_lane, down, up)

    h_right, h_left = pltpu.roll(after_v, 128 - 2 * DZ, 1), pltpu.roll(before_v, 126 - 2 * DZ, 1)
    rim = jnp.where(lane < 2, h_right, jnp.where(lane >= 126, h_left, 0.0))
    heat = jnp.concatenate([heat_ref[...], rim], axis=1)
    rates = []
    for z in range(3):
        k_right = pltpu.roll(after_k, (128 - 2 * z) % 128, 1)
        k_left = pltpu.roll(before_k, 126 - 2 * z, 1)
        k_rim = jnp.where(lane < 1, k_right, jnp.where(lane >= 127, k_left, 0.0))
        own = jnp.concatenate([diff_top[z], diff_rim[z * 8 : (z + 1) * 8, :]], axis=0)
        rates.append(jnp.concatenate([own, k_rim], axis=1))
    around = across(heat)
    first = heat + rates[0] * (2.0 * around - 16.0 * heat)
    second = rates[1] * around
    added = []
    for rate, own, p in (
        (rates[0], first, 2.0 * first + second),
        (rates[1], second, 2.0 * second + first),
        (rates[2], 0.0, second),
    ):
        added.append((own + rate * (across(p) - 16.0 * own))[:CX, :SB])

    left, right = left[:CX], right[:CX]
    edge = iota((CX, 128), 1)
    stores = []
    for n in range(CHUNKS):
        for z in range(n * some, (n + 1) * some):
            at_left = pltpu.roll(left, (128 - 2 * z) % 128, 1)
            at_right = pltpu.roll(right, 126 - 2 * z, 1)
            near = jnp.where(edge < 2, at_left, 0.0)
            far = jnp.where(edge >= 126, at_right, 0.0)
            step = jnp.concatenate([near, far], axis=1)
            if z < 3:
                step = step + added[z]
            out_ref[z] = base_ref[z] + step
        layers = pl.ds(n * some, some)
        stores.append(
            pltpu.make_async_copy(out_ref.at[layers], out_hbm.at[layers], out_sems.at[n])
        )
        stores[-1].start()
    for store in stores:
        store.wait()


def owner_kernel(
    got_hbm, face_hbm, flux_hbm, heat_hbm, even_hbm, odd_hbm,
    got_ref, face_ref, flux_ref, heat_ref, even_ref, odd_ref, sems, out_sems,
):
    rows = SPAN * PER // CHUNKS
    loads = [
        pltpu.make_async_copy(
            got_hbm.at[pl.ds(n * rows, rows)], got_ref.at[pl.ds(n * rows, rows)], sems.at[n]
        )
        for n in range(CHUNKS)
    ]
    loads.append(pltpu.make_async_copy(face_hbm, face_ref, sems.at[CHUNKS]))
    for load in loads:
        load.start()
    lane = iota((SPAN, 128), 1).astype(F32)
    for load in loads:
        load.wait()
    faces = jnp.concatenate([face_ref[...], jnp.zeros((128 - CX, SB), F32)], axis=0)
    codes = got_ref[pl.ds(4 * CAP, SPAN, stride=PER), :]
    onehot = jnp.concatenate(
        [jnp.where(codes[:, k : k + 1] == lane, 1.0, 0.0) for k in range(CAP)], axis=0
    ).astype(BF16)
    touched = pick(onehot, faces)

    def slots(c):
        return jnp.concatenate(
            [got_ref[pl.ds(k * 4 + c, SPAN, stride=PER), :] for k in range(CAP)], axis=0
        )

    temp = jnp.concatenate([slots(0), slots(1)], axis=1)
    gain = jnp.concatenate([slots(2), slots(3)], axis=1)
    flux = gain * (temp - touched)
    for k in range(CAP):
        for c in range(2):
            flux_ref[pl.ds(c * CAP + k, SPAN, stride=2 * CAP), :] = flux[
                k * SPAN : (k + 1) * SPAN, c * 128 : (c + 1) * 128
            ]
    store = pltpu.make_async_copy(flux_ref, flux_hbm, out_sems.at[3])
    store.start()
    heat = FACE_GAIN * pick(onehot, flux, (((0,), (0,)), ((), ())))[:CX]
    heat_ref[...] = heat
    is_even = lax.rem(lax.axis_index("span"), 2) == 0
    even_ref[...] = jnp.where(is_even, heat[CX - 8 :], heat[:8])
    odd_ref[...] = jnp.where(is_even, heat[:8], heat[CX - 8 :])
    small = [
        pltpu.make_async_copy(source, target, out_sems.at[n])
        for n, (source, target) in enumerate(
            ((heat_ref, heat_hbm), (even_ref, even_hbm), (odd_ref, odd_hbm))
        )
    ]
    for copy in small:
        copy.start()
    for copy in small:
        copy.wait()
    store.wait()


def heat_edges_kernel(
    heat_ref, even_in, odd_in, even_packed, odd_packed, rows_ref, even_ref, odd_ref
):
    span_even = lax.rem(lax.axis_index("span"), 2) == 0
    depth_even = lax.rem(lax.axis_index("depth"), 2) == 0
    below = jnp.where(span_even, even_in[...], odd_in[...])
    above = jnp.where(span_even, odd_in[...], even_in[...])
    sub = iota((8, SB), 0)
    rim = jnp.where(sub < 2, below, jnp.where(sub >= 6, above, 0.0))
    rows = jnp.concatenate([heat_ref[...], rim], axis=0)
    rows_ref[...] = rows
    here = lax.shift_right_logical(iota((EX, 128), 1), 1) == DZ
    left = pltpu.roll(rows[:, :128], 2 * DZ, 1)
    right = pltpu.roll(rows[:, 128:], 2 * DZ + 2, 1)
    for packed, out, one, other in (
        (even_packed, even_ref, right, left),
        (odd_packed, odd_ref, left, right),
    ):
        edge = jnp.where(depth_even, one, other)
        out[:EX, :128] = jnp.where(here, edge, packed[:EX, :128])
        out[:EX, 128:] = packed[:EX, 128:]
        out[EX:, :] = packed[EX:, :]


def shell_kernel(
    routes_ref, temp_ref, even_in, odd_in, flux_hbm, out_ref, flux_ref, sems
):
    some = SPAN // CHUNKS
    loads = [
        pltpu.make_async_copy(
            flux_hbm.at[pl.ds(n * some, some)], flux_ref.at[pl.ds(n * some, some)], sems.at[n]
        )
        for n in range(CHUNKS)
    ]
    for load in loads:
        load.start()
    depth_even = lax.rem(lax.axis_index("depth"), 2) == 0
    below = jnp.where(depth_even, even_in[EX : EX + 1, :], odd_in[EX : EX + 1, :])
    above = jnp.where(depth_even, odd_in[EX : EX + 1, :], even_in[EX : EX + 1, :])
    temp = temp_ref[...]
    sub, lane = iota((NB, SB), 0), iota((NB, SB), 1)
    upper = jnp.where(sub == 0, above, pltpu.roll(temp, 1, 0))
    lower = jnp.where(sub == NB - 1, below, pltpu.roll(temp, NB - 1, 0))
    before = jnp.where(lane == 0, 0.0, pltpu.roll(temp, 1, 1))
    after = jnp.where(lane == SB - 1, 0.0, pltpu.roll(temp, SB - 1, 1))
    laplace = lower + upper + after + before - 4.0 * temp
    out_ref[...] = temp + SHELL_RATE * laplace
    target = routes_ref[...].astype(F32)
    target_col = as_column(target, sub == lane)
    same = jnp.logical_and(target_col == target, lane < sub)
    rank_col = jnp.sum(jnp.where(same, 1.0, 0.0), axis=1, keepdims=True)
    position = (target_col * CAP + rank_col).astype(jnp.int32)
    slots = SLOTS // CHUNKS
    total = jnp.zeros((NB, SB), F32)
    for n in range(CHUNKS):
        take = jnp.where(iota((NB, slots), 1) + n * slots == position, 1.0, 0.0).astype(BF16)
        loads[n].wait()
        rows = slice(n * some, (n + 1) * some)
        flux = jnp.concatenate(
            [
                flux_ref[rows, c * CAP : (c + 1) * CAP, :].reshape(slots, 128)
                for c in range(2)
            ],
            axis=1,
        )
        total = total + pick(take, flux)
    out_ref[...] -= SHELL_SINK * total


def swap(even, odd, axis):
    size = lax.axis_size(axis)
    pairs = [(i, i ^ 1) for i in range(size)]
    shifted = [(i, ((i + 1) ^ 1) - 1) for i in range(1, size - 1)]
    return lax.ppermute(even, axis, pairs), lax.ppermute(odd, axis, shifted)


def local(shell_temp, contact_gain, die_temp, diffusivity, routes, tile_rows, closed):
    temp, gain = shell_temp[0], contact_gain[0]
    target = routes.reshape(1, NB)
    die, diff = die_temp.reshape(DZ * CX, SB), diffusivity.reshape(DZ * CX, SB)
    rows = jax.ShapeDtypeStruct((3 * DZ, SB), F32)
    even, odd = pl.pallas_call(
        edge_rows_kernel,
        out_shape=(rows, rows),
        grid=(1,),
        in_specs=[
            pl.BlockSpec((DZ, 8, SB), lambda i: (0, 0, 0)),
            pl.BlockSpec((DZ, 8, SB), lambda i: (0, CX // 8 - 1, 0)),
        ]
        * 2,
        out_specs=(VMEM,) * 2,
        compiler_params=params(60),
        name="edge_rows",
    )(die_temp, die_temp, diffusivity, diffusivity)
    sent = pl.pallas_call(
        pack_kernel,
        out_shape=pltpu.HBM((SPAN * PER, 128), F32),
        in_specs=[HBM] * 5,
        out_specs=HBM,
        scratch_shapes=[
            pltpu.VMEM((1, NB), jnp.int32),
            pltpu.VMEM((1, NB), jnp.int32),
            pltpu.VMEM((1, NB), jnp.int32),
            pltpu.VMEM((NB, SB), F32),
            pltpu.VMEM((NB, SB), F32),
            pltpu.VMEM((SPAN * PER, 128), F32),
            pltpu.SemaphoreType.DMA((5,)),
            pltpu.SemaphoreType.DMA((CHUNKS,)),
        ],
        compiler_params=params(60),
        cost_estimate=cost(6 * SLOTS * NB * 2 * SB, 4 * 2**20),
        name="pack",
    )(target, tile_rows, closed, temp, gain)
    got = lax.all_to_all(
        sent.reshape(SPAN * PER, 1, 128), "span", split_axis=0, concat_axis=0, tiled=True
    ).reshape(SPAN * PER, 128)
    even, odd = swap(even, odd, "span")
    columns, rim = pltpu.HBM((EX + 8, SB), F32), pltpu.HBM((DZ * 8, SB), F32)
    even_packed, odd_packed, die_rim, diff_rim, face = pl.pallas_call(
        edge_columns_kernel,
        out_shape=(columns, columns, rim, rim, pltpu.HBM((CX, SB), F32)),
        grid=(1,),
        in_specs=[VMEM] * 5,
        out_specs=(whole(EX + 8, SB),) * 2 + (whole(DZ * 8, SB),) * 2 + (whole(CX, SB),),
        compiler_params=params(16),
        name="edge_columns",
    )(die, diff, even, odd, temp)

    edge = pltpu.HBM((8, SB), F32)
    flux, heat, even, odd = pl.pallas_call(
        owner_kernel,
        out_shape=(
            pltpu.HBM((2 * SLOTS, 128), F32),
            pltpu.HBM((CX, SB), F32),
            edge,
            edge,
        ),
        grid=(1,),
        in_specs=[HBM] * 2,
        out_specs=(HBM,) * 4,
        scratch_shapes=[
            pltpu.VMEM((SPAN * PER, 128), F32),
            pltpu.VMEM((CX, SB), F32),
            pltpu.VMEM((2 * SLOTS, 128), F32),
            pltpu.VMEM((CX, SB), F32),
            pltpu.VMEM((8, SB), F32),
            pltpu.VMEM((8, SB), F32),
            pltpu.SemaphoreType.DMA((CHUNKS + 1,)),
            pltpu.SemaphoreType.DMA((4,)),
        ],
        compiler_params=params(60),
        name="owner",
    )(got, face)
    back = lax.all_to_all(
        flux.reshape(SPAN, 2 * CAP, 128), "span", split_axis=0, concat_axis=0, tiled=True
    )
    even, odd = swap(even, odd, "span")
    heat_rows, even, odd = pl.pallas_call(
        heat_edges_kernel,
        out_shape=(jax.ShapeDtypeStruct((EX, SB), F32),)
        + (jax.ShapeDtypeStruct((EX + 8, SB), F32),) * 2,
        in_specs=[VMEM] * 5,
        out_specs=(VMEM,) * 3,
        compiler_params=params(8),
        cost_estimate=cost(10**12, 2**32),
        name="heat_edges",
    )(heat, even, odd, even_packed, odd_packed)
    base = pl.pallas_call(
        sweeps_kernel,
        out_shape=jax.ShapeDtypeStruct((DZ, CX, SB), F32),
        grid=(1,),
        in_specs=[HBM, HBM, whole(DZ * 8, SB), whole(DZ * 8, SB), VMEM],
        out_specs=VMEM,
        scratch_shapes=[
            pltpu.VMEM((DZ * CX, SB), F32),
            pltpu.VMEM((DZ * CX, SB), F32),
            pltpu.VMEM((DZ + 2, EX, SB), F32),
            pltpu.VMEM((DZ + 2, EX, SB), F32),
            pltpu.VMEM((DZ, EX, SB), F32),
            pltpu.SemaphoreType.DMA((2 * CHUNKS,)),
        ],
        compiler_params=params(24),
        name="sweeps",
    )(die, diff, die_rim, diff_rim, heat_rows)
    even_own, odd_own = even, odd
    even, odd = swap(even, odd, "depth")
    die_next = pl.pallas_call(
        finish_kernel,
        out_shape=pltpu.HBM((DZ, CX, SB), F32),
        grid=(1,),
        in_specs=[
            VMEM,
            whole(3, CX, SB),
            pl.BlockSpec((24, SB), lambda i: (0, 0)),
        ]
        + [VMEM] * 5,
        out_specs=HBM,
        scratch_shapes=[
            pltpu.VMEM((DZ, CX, SB), F32),
            pltpu.SemaphoreType.DMA((CHUNKS,)),
        ],
        compiler_params=params(16),
        name="finish",
    )(base, diffusivity, diff_rim, heat_rows, even_own, odd_own, even, odd)
    shell_next = pl.pallas_call(
        shell_kernel,
        out_shape=pltpu.HBM((NB, SB), F32),
        grid=(1,),
        in_specs=[VMEM, VMEM, VMEM, VMEM, HBM],
        out_specs=whole(NB, SB),
        scratch_shapes=[
            pltpu.VMEM((SPAN, 2 * CAP, 128), F32),
            pltpu.SemaphoreType.DMA((CHUNKS,)),
        ],
        compiler_params=params(16),
        name="shell",
    )(target, temp, even, odd, back)
    return shell_next[None], die_next


def solution(mesh):
    placed = (
        P("span", "depth", None),
        P("span", "depth", None),
        P(None, "span", "depth"),
        P(None, "span", "depth"),
        P("span", "depth", None),
        P("span", "depth"),
        P("span", "depth"),
    )
    return jax.shard_map(
        local,
        mesh=mesh,
        in_specs=placed,
        out_specs=(P("span", "depth", None), P(None, "span", "depth")),
        check_vma=False,
    )
```

```python
import jax
import jax.numpy as jnp
from jax import lax
from jax.experimental import pallas as pl
from jax.experimental.pallas import tpu as pltpu
from jax.sharding import PartitionSpec as P

SHELL_RATE = 0.15
SHELL_SINK = 0.5
FACE_GAIN = 0.5
F32 = jnp.float32
BF16 = jnp.bfloat16

NB = 256
SB = 256
CX = 32
DZ = 48
CAP = 8
SPAN = 64
SLOTS = SPAN * CAP
PER = 4 * CAP + 1
EX = CX + 8
EY = SB + 128

CHUNKS = 4
PIECES = 1
UNROLL = 3
GROUP = 4

VMEM = pl.BlockSpec(memory_space=pltpu.VMEM)
HBM = pl.BlockSpec(memory_space=pltpu.HBM)
ANY = pl.BlockSpec(memory_space=pl.ANY)


def whole(*shape):
    return pl.BlockSpec(shape, lambda i: (0,) * len(shape))


def params(mib):
    return pltpu.CompilerParams(vmem_limit_bytes=mib * 2**20)


def cost(flops, moved):
    return pl.CostEstimate(flops=flops, bytes_accessed=moved, transcendentals=0)


def split(x):
    high = x.astype(BF16)
    return high, (x - high.astype(F32)).astype(BF16)


def pick(onehot, x, dims=(((1,), (0,)), ((), ()))):
    total = None
    for part in split(x):
        term = lax.dot_general(onehot, part, dims, preferred_element_type=F32)
        total = term if total is None else total + term
    return total


def iota(shape, dim):
    return lax.broadcasted_iota(jnp.int32, shape, dim)


def as_column(row, eye):
    return jnp.sum(jnp.where(eye, row, 0.0), axis=1, keepdims=True)


def pack_kernel(
    routes_hbm, tile_hbm, closed_hbm, temp_hbm, gain_hbm, out_hbm,
    routes_ref, tile_ref, closed_ref, temp_ref, gain_ref, out_ref, sems, out_sems,
):
    loads = [
        pltpu.make_async_copy(source, target, sems.at[n])
        for n, (source, target) in enumerate(
            (
                (routes_hbm, routes_ref),
                (tile_hbm, tile_ref),
                (closed_hbm, closed_ref),
                (temp_hbm, temp_ref),
                (gain_hbm, gain_ref),
            )
        )
    ]
    for load in loads:
        load.start()
    sub, lane = iota((NB, NB), 0), iota((NB, NB), 1)
    eye = sub == lane
    for load in loads[:3]:
        load.wait()
    target = routes_ref[...].astype(F32)
    same = as_column(target, eye) == target
    rank_row = jnp.sum(
        jnp.where(jnp.logical_and(same, sub < lane), 1.0, 0.0), axis=0, keepdims=True
    )
    rank_col = jnp.sum(
        jnp.where(jnp.logical_and(same, lane < sub), 1.0, 0.0), axis=1, keepdims=True
    )
    tile_col = as_column(tile_ref[...].astype(F32), eye)
    closed_col = as_column(closed_ref[...].astype(F32), eye)
    position = (target * CAP + rank_row).astype(jnp.int32)
    codes = lax.dot_general(
        jnp.where(iota((SPAN, NB), 0) == routes_ref[...], 1.0, 0.0).astype(BF16),
        jnp.where(iota((NB, 128), 1) == rank_col.astype(jnp.int32), tile_col, 0.0).astype(BF16),
        (((1,), (0,)), ((), ())),
        preferred_element_type=F32,
    )
    out_ref[pl.ds(4 * CAP, SPAN, stride=PER), :] = codes
    for load in loads[3:]:
        load.wait()
    parts = split(jnp.concatenate([temp_ref[...], gain_ref[...] * closed_col], axis=1))
    chunk = SPAN // CHUNKS
    stores = []
    for g in range(CHUNKS):
        first = g * chunk * CAP
        put = jnp.where(iota((chunk * CAP, NB), 0) + first == position, 1.0, 0.0).astype(BF16)
        slots = sum(jnp.dot(put, part, preferred_element_type=F32) for part in parts)
        for c in range(4):
            for t in range(chunk):
                out_ref[pl.ds((g * chunk + t) * PER + c, CAP, stride=4), :] = slots[
                    t * CAP : (t + 1) * CAP, c * 128 : (c + 1) * 128
                ]
        rows = pl.ds(g * chunk * PER, chunk * PER)
        stores.append(pltpu.make_async_copy(out_ref.at[rows], out_hbm.at[rows], out_sems.at[g]))
        stores[-1].start()
    for store in stores:
        store.wait()


def edge_rows_kernel(die_first, die_last, diff_first, diff_last, even_ref, odd_ref):
    is_even = lax.rem(lax.axis_index("span"), 2) == 0

    def layer(z, carry):
        for n, (first, low, last, high) in enumerate(
            ((die_first, 0, die_last, 6), (die_first, 1, die_last, 7), (diff_first, 0, diff_last, 7))
        ):
            top = first[z, low : low + 1, :]
            bottom = last[z, high : high + 1, :]
            even_ref[pl.ds(n * DZ + z, 1), :] = jnp.where(is_even, bottom, top)
            odd_ref[pl.ds(n * DZ + z, 1), :] = jnp.where(is_even, top, bottom)
        return carry

    lax.fori_loop(0, DZ, layer, 0, unroll=8)


def edge_columns_kernel(
    die_ref, diff_ref, even_in, odd_in, temp_ref, even_ref, odd_ref, die_rim, diff_rim, face_ref
):
    span_even = lax.rem(lax.axis_index("span"), 2) == 0
    depth_even = lax.rem(lax.axis_index("depth"), 2) == 0
    sub = iota((8, SB), 0)

    def rim_of(z, spots):
        tile = jnp.zeros((8, SB), F32)
        for spot, n, up in spots:
            at = pl.ds(n * DZ + z, 1)
            row = jnp.where(span_even != up, even_in[at, :], odd_in[at, :])
            tile = jnp.where(sub == spot, row, tile)
        return tile

    lane = iota((EX, 128), 1)

    def add_layer(z, kept):
        v_left, v_right, k_left, k_right = kept
        rows, rim = pl.ds(pl.multiple_of(z * CX, CX), CX), pl.ds(pl.multiple_of(z * 8, 8), 8)
        v_rim = rim_of(z, ((0, 0, False), (1, 1, False), (6, 0, True), (7, 1, True)))
        k_rim = rim_of(z, ((0, 2, False), (7, 2, True)))
        die_rim[rim, :] = v_rim
        diff_rim[rim, :] = k_rim
        v = jnp.concatenate([die_ref[rows, :], v_rim], axis=0)
        k = jnp.concatenate([diff_ref[rows, :], k_rim], axis=0)
        here = lax.shift_right_logical(lane, 1) == z
        v_left = jnp.where(here, pltpu.roll(v[:, :128], 2 * z, 1), v_left)
        v_right = jnp.where(here, pltpu.roll(v[:, 128:], 2 * z + 2, 1), v_right)
        k_left = jnp.where(here, pltpu.roll(k[:, :128], 2 * z, 1), k_left)
        k_right = jnp.where(here, pltpu.roll(k[:, 128:], 2 * z + 2, 1), k_right)
        return v_left, v_right, k_left, k_right

    none = jnp.zeros((EX, 128), F32)
    v_left, v_right, k_left, k_right = lax.fori_loop(0, DZ, add_layer, (none,) * 4, unroll=8)
    even_ref[:EX, :128] = jnp.where(depth_even, v_right, v_left)
    even_ref[:EX, 128:] = jnp.where(depth_even, k_right, k_left)
    odd_ref[:EX, :128] = jnp.where(depth_even, v_left, v_right)
    odd_ref[:EX, 128:] = jnp.where(depth_even, k_left, k_right)
    first, last = temp_ref[0:1, :], temp_ref[NB - 1 : NB, :]
    even_ref[EX:, :] = jnp.broadcast_to(jnp.where(depth_even, last, first), (8, SB))
    odd_ref[EX:, :] = jnp.broadcast_to(jnp.where(depth_even, first, last), (8, SB))
    face_ref[...] = die_ref[:CX, :]


def across(p):
    q = p + 0.5 * (pltpu.roll(p, 1, 1) + pltpu.roll(p, p.shape[1] - 1, 1))
    return q + 0.5 * (pltpu.roll(q, 1, 0) + pltpu.roll(q, q.shape[0] - 1, 0))


def sweeps_kernel(
    die_hbm, diff_hbm, die_rim, diff_rim, after_ref, out_ref,
    die_ref, diff_ref, field, later, rate, sems,
):
    del after_ref
    some = DZ // CHUNKS
    loads = []
    for n in range(CHUNKS):
        for m, (source, target) in enumerate(((die_hbm, die_ref), (diff_hbm, diff_ref))):
            rows = pl.ds(n * some * CX, some * CX)
            loads.append(
                pltpu.make_async_copy(source.at[rows], target.at[rows], sems.at[2 * n + m])
            )
            loads[-1].start()
    none = jnp.zeros((EX, SB), F32)
    for ref in (field, later):
        ref[0] = none
        ref[DZ + 1] = none
    for n in range(CHUNKS):
        loads[2 * n].wait()
        loads[2 * n + 1].wait()
        for z in range(n * some, (n + 1) * some):
            field[z + 1, :CX] = die_ref[z * CX : (z + 1) * CX, :]
            field[z + 1, CX:] = die_rim[z * 8 : (z + 1) * 8, :]
            rate[z, :CX] = diff_ref[z * CX : (z + 1) * CX, :]
            rate[z, CX:] = diff_rim[z * 8 : (z + 1) * 8, :]
    gap = jnp.abs(iota((SB, SB), 0) - iota((SB, SB), 1))
    band = jnp.where(gap == 0, 1.0, jnp.where(gap == 1, 0.5, 0.0)).astype(BF16)

    def around(ref, start):
        layers = []
        for n in range(GROUP):
            z = start + n
            layers.append(2.0 * ref[z + 1] + (ref[z] + ref[z + 2]))
        p = jnp.concatenate(layers, axis=0)
        high, low = split(p)
        q = jnp.dot(high, band, preferred_element_type=F32)
        q = q + jnp.dot(low, band, preferred_element_type=F32)
        for n in range(GROUP):
            own = q[n * EX : (n + 1) * EX]
            yield own + 0.5 * (pltpu.roll(own, 1, 0) + pltpu.roll(own, EX - 1, 0))

    def first(g, carry):
        for n, q in enumerate(around(field, g * GROUP)):
            z = g * GROUP + n
            v = field[z + 1]
            later[z + 1] = v + rate[z] * (q - 16.0 * v)
        return carry

    lax.fori_loop(0, DZ // GROUP, first, 0, unroll=4 * UNROLL)

    def second(g, carry):
        for n, q in enumerate(around(later, g * GROUP)):
            z = g * GROUP + n
            v = later[z + 1, :CX]
            out_ref[z] = v + rate[z, :CX] * (q[:CX] - 16.0 * v)
        return carry

    lax.fori_loop(0, DZ // GROUP, second, 0, unroll=4 * UNROLL)


def smooth(x):
    z = 2.0 * x + (pltpu.roll(x, 2, 1) + pltpu.roll(x, 126, 1))
    return z + 0.5 * (pltpu.roll(z, 1, 0) + pltpu.roll(z, EX - 1, 0))


def finish_kernel(
    base_ref, diff_top, diff_rim, heat_ref, even_own, odd_own, even_in, odd_in, out_hbm,
    out_ref, out_sems,
):
    some = DZ // CHUNKS
    depth_even = lax.rem(lax.axis_index("depth"), 2) == 0
    lane = iota((EX, 128), 1)
    die = lane < 2 * DZ
    first_lane = jnp.logical_and(die, lax.rem(lane, 2) == 0)
    second_lane = jnp.logical_and(die, lax.rem(lane, 2) == 1)

    def parts(even_ref, odd_ref, when):
        v = jnp.where(when, even_ref[:EX, :128], odd_ref[:EX, :128])
        return v, jnp.where(when, even_ref[:EX, 128:], odd_ref[:EX, 128:])

    right_v, right_k = parts(even_own, odd_own, depth_even)
    left_v, left_k = parts(even_own, odd_own, jnp.logical_not(depth_even))
    after_v, after_k = parts(even_in, odd_in, depth_even)
    before_v, before_k = parts(even_in, odd_in, jnp.logical_not(depth_even))

    def up(x):
        return pltpu.roll(x, 1, 1)

    def down(x):
        return pltpu.roll(x, 127, 1)

    def change(own_v, own_k, out_v, out_k, outer, inner, to_outer, to_inner):
        own_w, out_w = smooth(jnp.where(die, own_v, 0.0)), smooth(jnp.where(die, out_v, 0.0))
        near = out_v + out_k * (
            out_w + 0.5 * (to_outer(out_w) + to_outer(own_w)) - 16.0 * out_v
        )
        near = jnp.where(outer, near, 0.0)
        moved = jnp.where(inner, 0.5 * own_k * to_inner(out_w), 0.0)
        spread = smooth(moved)
        edge = moved + own_k * (spread - 16.0 * moved + 0.5 * to_inner(smooth(near)))
        return jnp.where(inner, edge, jnp.where(die, 0.5 * own_k * to_outer(spread), 0.0))

    left = change(left_v, left_k, before_v, before_k, second_lane, first_lane, up, down)
    right = change(right_v, right_k, after_v, after_k, first_lane, second_lane, down, up)

    h_right, h_left = pltpu.roll(after_v, 128 - 2 * DZ, 1), pltpu.roll(before_v, 126 - 2 * DZ, 1)
    rim = jnp.where(lane < 2, h_right, jnp.where(lane >= 126, h_left, 0.0))
    heat = jnp.concatenate([heat_ref[...], rim], axis=1)
    rates = []
    for z in range(3):
        k_right = pltpu.roll(after_k, (128 - 2 * z) % 128, 1)
        k_left = pltpu.roll(before_k, 126 - 2 * z, 1)
        k_rim = jnp.where(lane < 1, k_right, jnp.where(lane >= 127, k_left, 0.0))
        own = jnp.concatenate([diff_top[z], diff_rim[z * 8 : (z + 1) * 8, :]], axis=0)
        rates.append(jnp.concatenate([own, k_rim], axis=1))
    around = across(heat)
    first = heat + rates[0] * (2.0 * around - 16.0 * heat)
    second = rates[1] * around
    added = []
    for rate, own, p in (
        (rates[0], first, 2.0 * first + second),
        (rates[1], second, 2.0 * second + first),
        (rates[2], 0.0, second),
    ):
        added.append((own + rate * (across(p) - 16.0 * own))[:CX, :SB])

    left, right = left[:CX], right[:CX]
    edge = iota((CX, 128), 1)
    stores = []
    for n in range(CHUNKS):
        for z in range(n * some, (n + 1) * some):
            at_left = pltpu.roll(left, (128 - 2 * z) % 128, 1)
            at_right = pltpu.roll(right, 126 - 2 * z, 1)
            near = jnp.where(edge < 2, at_left, 0.0)
            far = jnp.where(edge >= 126, at_right, 0.0)
            step = jnp.concatenate([near, far], axis=1)
            if z < 3:
                step = step + added[z]
            out_ref[z] = base_ref[z] + step
        layers = pl.ds(n * some, some)
        stores.append(
            pltpu.make_async_copy(out_ref.at[layers], out_hbm.at[layers], out_sems.at[n])
        )
        stores[-1].start()
    for store in stores:
        store.wait()


def owner_kernel(
    got_hbm, face_hbm, flux_hbm, heat_hbm, even_hbm, odd_hbm,
    got_ref, face_ref, flux_ref, heat_ref, even_ref, odd_ref, sems, out_sems,
):
    rows = SPAN * PER // CHUNKS
    loads = [
        pltpu.make_async_copy(
            got_hbm.at[pl.ds(n * rows, rows)], got_ref.at[pl.ds(n * rows, rows)], sems.at[n]
        )
        for n in range(CHUNKS)
    ]
    loads.append(pltpu.make_async_copy(face_hbm, face_ref, sems.at[CHUNKS]))
    for load in loads:
        load.start()
    lane = iota((SPAN, 128), 1).astype(F32)
    for load in loads:
        load.wait()
    faces = jnp.concatenate([face_ref[...], jnp.zeros((128 - CX, SB), F32)], axis=0)
    codes = got_ref[pl.ds(4 * CAP, SPAN, stride=PER), :]
    onehot = jnp.concatenate(
        [jnp.where(codes[:, k : k + 1] == lane, 1.0, 0.0) for k in range(CAP)], axis=0
    ).astype(BF16)
    touched = pick(onehot, faces)

    def slots(c):
        return jnp.concatenate(
            [got_ref[pl.ds(k * 4 + c, SPAN, stride=PER), :] for k in range(CAP)], axis=0
        )

    temp = jnp.concatenate([slots(0), slots(1)], axis=1)
    gain = jnp.concatenate([slots(2), slots(3)], axis=1)
    flux = gain * (temp - touched)
    for k in range(CAP):
        for c in range(2):
            flux_ref[pl.ds(c * CAP + k, SPAN, stride=2 * CAP), :] = flux[
                k * SPAN : (k + 1) * SPAN, c * 128 : (c + 1) * 128
            ]
    store = pltpu.make_async_copy(flux_ref, flux_hbm, out_sems.at[3])
    store.start()
    heat = FACE_GAIN * pick(onehot, flux, (((0,), (0,)), ((), ())))[:CX]
    heat_ref[...] = heat
    is_even = lax.rem(lax.axis_index("span"), 2) == 0
    even_ref[...] = jnp.where(is_even, heat[CX - 8 :], heat[:8])
    odd_ref[...] = jnp.where(is_even, heat[:8], heat[CX - 8 :])
    small = [
        pltpu.make_async_copy(source, target, out_sems.at[n])
        for n, (source, target) in enumerate(
            ((heat_ref, heat_hbm), (even_ref, even_hbm), (odd_ref, odd_hbm))
        )
    ]
    for copy in small:
        copy.start()
    for copy in small:
        copy.wait()
    store.wait()


def heat_edges_kernel(
    heat_ref, even_in, odd_in, even_packed, odd_packed, rows_ref, even_ref, odd_ref
):
    span_even = lax.rem(lax.axis_index("span"), 2) == 0
    depth_even = lax.rem(lax.axis_index("depth"), 2) == 0
    below = jnp.where(span_even, even_in[...], odd_in[...])
    above = jnp.where(span_even, odd_in[...], even_in[...])
    sub = iota((8, SB), 0)
    rim = jnp.where(sub < 2, below, jnp.where(sub >= 6, above, 0.0))
    rows = jnp.concatenate([heat_ref[...], rim], axis=0)
    rows_ref[...] = rows
    here = lax.shift_right_logical(iota((EX, 128), 1), 1) == DZ
    left = pltpu.roll(rows[:, :128], 2 * DZ, 1)
    right = pltpu.roll(rows[:, 128:], 2 * DZ + 2, 1)
    for packed, out, one, other in (
        (even_packed, even_ref, right, left),
        (odd_packed, odd_ref, left, right),
    ):
        edge = jnp.where(depth_even, one, other)
        out[:EX, :128] = jnp.where(here, edge, packed[:EX, :128])
        out[:EX, 128:] = packed[:EX, 128:]
        out[EX:, :] = packed[EX:, :]


def shell_kernel(
    routes_ref, temp_ref, even_in, odd_in, flux_hbm, out_ref, flux_ref, sems
):
    some = SPAN // PIECES
    loads = [
        pltpu.make_async_copy(
            flux_hbm.at[pl.ds(n * some, some)], flux_ref.at[pl.ds(n * some, some)], sems.at[n]
        )
        for n in range(PIECES)
    ]
    for load in loads:
        load.start()
    depth_even = lax.rem(lax.axis_index("depth"), 2) == 0
    below = jnp.where(depth_even, even_in[EX : EX + 1, :], odd_in[EX : EX + 1, :])
    above = jnp.where(depth_even, odd_in[EX : EX + 1, :], even_in[EX : EX + 1, :])
    temp = temp_ref[...]
    sub, lane = iota((NB, SB), 0), iota((NB, SB), 1)
    upper = jnp.where(sub == 0, above, pltpu.roll(temp, 1, 0))
    lower = jnp.where(sub == NB - 1, below, pltpu.roll(temp, NB - 1, 0))
    before = jnp.where(lane == 0, 0.0, pltpu.roll(temp, 1, 1))
    after = jnp.where(lane == SB - 1, 0.0, pltpu.roll(temp, SB - 1, 1))
    laplace = lower + upper + after + before - 4.0 * temp
    out_ref[...] = temp + SHELL_RATE * laplace
    target = routes_ref[...].astype(F32)
    target_col = as_column(target, sub == lane)
    same = jnp.logical_and(target_col == target, lane < sub)
    rank_col = jnp.sum(jnp.where(same, 1.0, 0.0), axis=1, keepdims=True)
    position = (target_col * CAP + rank_col).astype(jnp.int32)
    slots = SLOTS // PIECES
    total = jnp.zeros((NB, SB), F32)
    for n in range(PIECES):
        take = jnp.where(iota((NB, slots), 1) + n * slots == position, 1.0, 0.0).astype(BF16)
        loads[n].wait()
        rows = slice(n * some, (n + 1) * some)
        flux = jnp.concatenate(
            [
                flux_ref[rows, c * CAP : (c + 1) * CAP, :].reshape(slots, 128)
                for c in range(2)
            ],
            axis=1,
        )
        total = total + pick(take, flux)
    out_ref[...] -= SHELL_SINK * total


def swap(even, odd, axis):
    size = lax.axis_size(axis)
    pairs = [(i, i ^ 1) for i in range(size)]
    shifted = [(i, ((i + 1) ^ 1) - 1) for i in range(1, size - 1)]
    return lax.ppermute(even, axis, pairs), lax.ppermute(odd, axis, shifted)


def local(shell_temp, contact_gain, die_temp, diffusivity, routes, tile_rows, closed):
    temp, gain = shell_temp[0], contact_gain[0]
    target = routes.reshape(1, NB)
    die, diff = die_temp.reshape(DZ * CX, SB), diffusivity.reshape(DZ * CX, SB)
    rows = jax.ShapeDtypeStruct((3 * DZ, SB), F32)
    even, odd = pl.pallas_call(
        edge_rows_kernel,
        out_shape=(rows, rows),
        grid=(1,),
        in_specs=[
            pl.BlockSpec((DZ, 8, SB), lambda i: (0, 0, 0)),
            pl.BlockSpec((DZ, 8, SB), lambda i: (0, CX // 8 - 1, 0)),
        ]
        * 2,
        out_specs=(VMEM,) * 2,
        compiler_params=params(60),
        name="edge_rows",
    )(die_temp, die_temp, diffusivity, diffusivity)
    sent = pl.pallas_call(
        pack_kernel,
        out_shape=pltpu.HBM((SPAN * PER, 128), F32),
        in_specs=[HBM] * 5,
        out_specs=HBM,
        scratch_shapes=[
            pltpu.VMEM((1, NB), jnp.int32),
            pltpu.VMEM((1, NB), jnp.int32),
            pltpu.VMEM((1, NB), jnp.int32),
            pltpu.VMEM((NB, SB), F32),
            pltpu.VMEM((NB, SB), F32),
            pltpu.VMEM((SPAN * PER, 128), F32),
            pltpu.SemaphoreType.DMA((5,)),
            pltpu.SemaphoreType.DMA((CHUNKS,)),
        ],
        compiler_params=params(60),
        cost_estimate=cost(6 * SLOTS * NB * 2 * SB, 4 * 2**20),
        name="pack",
    )(target, tile_rows, closed, temp, gain)
    got = lax.all_to_all(
        sent.reshape(SPAN * PER, 1, 128), "span", split_axis=0, concat_axis=0, tiled=True
    ).reshape(SPAN * PER, 128)
    even, odd = swap(even, odd, "span")
    columns, rim = pltpu.HBM((EX + 8, SB), F32), pltpu.HBM((DZ * 8, SB), F32)
    even_packed, odd_packed, die_rim, diff_rim, face = pl.pallas_call(
        edge_columns_kernel,
        out_shape=(columns, columns, rim, rim, pltpu.HBM((CX, SB), F32)),
        grid=(1,),
        in_specs=[VMEM] * 5,
        out_specs=(whole(EX + 8, SB),) * 2 + (whole(DZ * 8, SB),) * 2 + (whole(CX, SB),),
        compiler_params=params(16),
        name="edge_columns",
    )(die, diff, even, odd, temp)

    edge = pltpu.HBM((8, SB), F32)
    flux, heat, even, odd = pl.pallas_call(
        owner_kernel,
        out_shape=(
            pltpu.HBM((2 * SLOTS, 128), F32),
            pltpu.HBM((CX, SB), F32),
            edge,
            edge,
        ),
        grid=(1,),
        in_specs=[HBM] * 2,
        out_specs=(HBM,) * 4,
        scratch_shapes=[
            pltpu.VMEM((SPAN * PER, 128), F32),
            pltpu.VMEM((CX, SB), F32),
            pltpu.VMEM((2 * SLOTS, 128), F32),
            pltpu.VMEM((CX, SB), F32),
            pltpu.VMEM((8, SB), F32),
            pltpu.VMEM((8, SB), F32),
            pltpu.SemaphoreType.DMA((CHUNKS + 1,)),
            pltpu.SemaphoreType.DMA((4,)),
        ],
        compiler_params=params(60),
        name="owner",
    )(got, face)
    back = lax.all_to_all(
        flux.reshape(SPAN, 2 * CAP, 128), "span", split_axis=0, concat_axis=0, tiled=True
    )
    even, odd = swap(even, odd, "span")
    heat_rows, even, odd = pl.pallas_call(
        heat_edges_kernel,
        out_shape=(jax.ShapeDtypeStruct((EX, SB), F32),)
        + (jax.ShapeDtypeStruct((EX + 8, SB), F32),) * 2,
        in_specs=[VMEM] * 5,
        out_specs=(VMEM,) * 3,
        compiler_params=params(8),
        cost_estimate=cost(10**12, 2**32),
        name="heat_edges",
    )(heat, even, odd, even_packed, odd_packed)
    base = pl.pallas_call(
        sweeps_kernel,
        out_shape=jax.ShapeDtypeStruct((DZ, CX, SB), F32),
        grid=(1,),
        in_specs=[HBM, HBM, whole(DZ * 8, SB), whole(DZ * 8, SB), VMEM],
        out_specs=VMEM,
        scratch_shapes=[
            pltpu.VMEM((DZ * CX, SB), F32),
            pltpu.VMEM((DZ * CX, SB), F32),
            pltpu.VMEM((DZ + 2, EX, SB), F32),
            pltpu.VMEM((DZ + 2, EX, SB), F32),
            pltpu.VMEM((DZ, EX, SB), F32),
            pltpu.SemaphoreType.DMA((2 * CHUNKS,)),
        ],
        compiler_params=params(24),
        name="sweeps",
    )(die, diff, die_rim, diff_rim, heat_rows)
    even_own, odd_own = even, odd
    even, odd = swap(even, odd, "depth")
    die_next = pl.pallas_call(
        finish_kernel,
        out_shape=pltpu.HBM((DZ, CX, SB), F32),
        grid=(1,),
        in_specs=[
            VMEM,
            whole(3, CX, SB),
            pl.BlockSpec((24, SB), lambda i: (0, 0)),
        ]
        + [VMEM] * 5,
        out_specs=HBM,
        scratch_shapes=[
            pltpu.VMEM((DZ, CX, SB), F32),
            pltpu.SemaphoreType.DMA((CHUNKS,)),
        ],
        compiler_params=params(16),
        name="finish",
    )(base, diffusivity, diff_rim, heat_rows, even_own, odd_own, even, odd)
    shell_next = pl.pallas_call(
        shell_kernel,
        out_shape=pltpu.HBM((NB, SB), F32),
        grid=(1,),
        in_specs=[VMEM, VMEM, VMEM, VMEM, HBM],
        out_specs=whole(NB, SB),
        scratch_shapes=[
            pltpu.VMEM((SPAN, 2 * CAP, 128), F32),
            pltpu.SemaphoreType.DMA((PIECES,)),
        ],
        compiler_params=params(16),
        name="shell",
    )(target, temp, even, odd, back)
    return shell_next[None], die_next


def solution(mesh):
    placed = (
        P("span", "depth", None),
        P("span", "depth", None),
        P(None, "span", "depth"),
        P(None, "span", "depth"),
        P("span", "depth", None),
        P("span", "depth"),
        P("span", "depth"),
    )
    return jax.shard_map(
        local,
        mesh=mesh,
        in_specs=placed,
        out_specs=(P("span", "depth", None), P(None, "span", "depth")),
        check_vma=False,
    )
```

```python
import jax
import jax.numpy as jnp
from jax import lax
from jax.experimental import pallas as pl
from jax.experimental.pallas import tpu as pltpu
from jax.sharding import PartitionSpec as P

SHELL_RATE = 0.15
SHELL_SINK = 0.5
FACE_GAIN = 0.5
F32 = jnp.float32
BF16 = jnp.bfloat16

NB = 256
SB = 256
CX = 32
DZ = 48
CAP = 8
SPAN = 64
SLOTS = SPAN * CAP
PER = 4 * CAP + 1
EX = CX + 8
EY = SB + 128

CHUNKS = 4
PIECES = 1
UNROLL = 3
GROUP = 4

VMEM = pl.BlockSpec(memory_space=pltpu.VMEM)
HBM = pl.BlockSpec(memory_space=pltpu.HBM)
ANY = pl.BlockSpec(memory_space=pl.ANY)


def whole(*shape):
    return pl.BlockSpec(shape, lambda i: (0,) * len(shape))


def params(mib):
    return pltpu.CompilerParams(vmem_limit_bytes=mib * 2**20)


def cost(flops, moved):
    return pl.CostEstimate(flops=flops, bytes_accessed=moved, transcendentals=0)


def split(x):
    high = x.astype(BF16)
    return high, (x - high.astype(F32)).astype(BF16)


def pick(onehot, x, dims=(((1,), (0,)), ((), ()))):
    total = None
    for part in split(x):
        term = lax.dot_general(onehot, part, dims, preferred_element_type=F32)
        total = term if total is None else total + term
    return total


def iota(shape, dim):
    return lax.broadcasted_iota(jnp.int32, shape, dim)


def as_column(row, eye):
    return jnp.sum(jnp.where(eye, row, 0.0), axis=1, keepdims=True)


def pack_kernel(
    routes_hbm, tile_hbm, closed_hbm, temp_hbm, gain_hbm, out_hbm,
    routes_ref, tile_ref, closed_ref, temp_ref, gain_ref, out_ref, sems, out_sems,
):
    loads = [
        pltpu.make_async_copy(source, target, sems.at[n])
        for n, (source, target) in enumerate(
            (
                (routes_hbm, routes_ref),
                (tile_hbm, tile_ref),
                (closed_hbm, closed_ref),
                (temp_hbm, temp_ref),
                (gain_hbm, gain_ref),
            )
        )
    ]
    for load in loads:
        load.start()
    sub, lane = iota((NB, NB), 0), iota((NB, NB), 1)
    eye = sub == lane
    for load in loads[:3]:
        load.wait()
    target = routes_ref[...].astype(F32)
    same = as_column(target, eye) == target
    rank_row = jnp.sum(
        jnp.where(jnp.logical_and(same, sub < lane), 1.0, 0.0), axis=0, keepdims=True
    )
    rank_col = jnp.sum(
        jnp.where(jnp.logical_and(same, lane < sub), 1.0, 0.0), axis=1, keepdims=True
    )
    tile_col = as_column(tile_ref[...].astype(F32), eye)
    closed_col = as_column(closed_ref[...].astype(F32), eye)
    position = (target * CAP + rank_row).astype(jnp.int32)
    codes = lax.dot_general(
        jnp.where(iota((SPAN, NB), 0) == routes_ref[...], 1.0, 0.0).astype(BF16),
        jnp.where(iota((NB, 128), 1) == rank_col.astype(jnp.int32), tile_col, 0.0).astype(BF16),
        (((1,), (0,)), ((), ())),
        preferred_element_type=F32,
    )
    out_ref[pl.ds(4 * CAP, SPAN, stride=PER), :] = codes
    for load in loads[3:]:
        load.wait()
    parts = split(jnp.concatenate([temp_ref[...], gain_ref[...] * closed_col], axis=1))
    chunk = SPAN // CHUNKS
    stores = []
    for g in range(CHUNKS):
        first = g * chunk * CAP
        put = jnp.where(iota((chunk * CAP, NB), 0) + first == position, 1.0, 0.0).astype(BF16)
        slots = sum(jnp.dot(put, part, preferred_element_type=F32) for part in parts)
        for c in range(4):
            for t in range(chunk):
                out_ref[pl.ds((g * chunk + t) * PER + c, CAP, stride=4), :] = slots[
                    t * CAP : (t + 1) * CAP, c * 128 : (c + 1) * 128
                ]
        rows = pl.ds(g * chunk * PER, chunk * PER)
        stores.append(pltpu.make_async_copy(out_ref.at[rows], out_hbm.at[rows], out_sems.at[g]))
        stores[-1].start()
    for store in stores:
        store.wait()


def edge_rows_kernel(die_first, die_last, diff_first, diff_last, even_ref, odd_ref):
    is_even = lax.rem(lax.axis_index("span"), 2) == 0

    def layer(z, carry):
        for n, (first, low, last, high) in enumerate(
            ((die_first, 0, die_last, 6), (die_first, 1, die_last, 7), (diff_first, 0, diff_last, 7))
        ):
            top = first[z, low : low + 1, :]
            bottom = last[z, high : high + 1, :]
            even_ref[pl.ds(n * DZ + z, 1), :] = jnp.where(is_even, bottom, top)
            odd_ref[pl.ds(n * DZ + z, 1), :] = jnp.where(is_even, top, bottom)
        return carry

    lax.fori_loop(0, DZ, layer, 0, unroll=8)


def edge_columns_kernel(
    die_ref, diff_ref, even_in, odd_in, temp_ref, even_ref, odd_ref, die_rim, diff_rim, face_ref
):
    span_even = lax.rem(lax.axis_index("span"), 2) == 0
    depth_even = lax.rem(lax.axis_index("depth"), 2) == 0
    sub = iota((8, SB), 0)

    def rim_of(z, spots):
        tile = jnp.zeros((8, SB), F32)
        for spot, n, up in spots:
            at = pl.ds(n * DZ + z, 1)
            row = jnp.where(span_even != up, even_in[at, :], odd_in[at, :])
            tile = jnp.where(sub == spot, row, tile)
        return tile

    lane = iota((EX, 128), 1)

    def add_layer(z, kept):
        v_left, v_right, k_left, k_right = kept
        rows, rim = pl.ds(pl.multiple_of(z * CX, CX), CX), pl.ds(pl.multiple_of(z * 8, 8), 8)
        v_rim = rim_of(z, ((0, 0, False), (1, 1, False), (6, 0, True), (7, 1, True)))
        k_rim = rim_of(z, ((0, 2, False), (7, 2, True)))
        die_rim[rim, :] = v_rim
        diff_rim[rim, :] = k_rim
        v = jnp.concatenate([die_ref[rows, :], v_rim], axis=0)
        k = jnp.concatenate([diff_ref[rows, :], k_rim], axis=0)
        here = lax.shift_right_logical(lane, 1) == z
        v_left = jnp.where(here, pltpu.roll(v[:, :128], 2 * z, 1), v_left)
        v_right = jnp.where(here, pltpu.roll(v[:, 128:], 2 * z + 2, 1), v_right)
        k_left = jnp.where(here, pltpu.roll(k[:, :128], 2 * z, 1), k_left)
        k_right = jnp.where(here, pltpu.roll(k[:, 128:], 2 * z + 2, 1), k_right)
        return v_left, v_right, k_left, k_right

    none = jnp.zeros((EX, 128), F32)
    v_left, v_right, k_left, k_right = lax.fori_loop(0, DZ, add_layer, (none,) * 4, unroll=8)
    even_ref[:EX, :128] = jnp.where(depth_even, v_right, v_left)
    even_ref[:EX, 128:] = jnp.where(depth_even, k_right, k_left)
    odd_ref[:EX, :128] = jnp.where(depth_even, v_left, v_right)
    odd_ref[:EX, 128:] = jnp.where(depth_even, k_left, k_right)
    first, last = temp_ref[0:1, :], temp_ref[NB - 1 : NB, :]
    even_ref[EX:, :] = jnp.broadcast_to(jnp.where(depth_even, last, first), (8, SB))
    odd_ref[EX:, :] = jnp.broadcast_to(jnp.where(depth_even, first, last), (8, SB))
    face_ref[...] = die_ref[:CX, :]


def across(p):
    q = p + 0.5 * (pltpu.roll(p, 1, 1) + pltpu.roll(p, p.shape[1] - 1, 1))
    return q + 0.5 * (pltpu.roll(q, 1, 0) + pltpu.roll(q, q.shape[0] - 1, 0))


def sweeps_kernel(
    die_hbm, diff_hbm, die_rim, diff_rim, after_ref, out_ref,
    die_ref, diff_ref, field, later, rate, sems,
):
    del after_ref
    some = DZ // CHUNKS
    loads = []
    for n in range(CHUNKS):
        for m, (source, target) in enumerate(((die_hbm, die_ref), (diff_hbm, diff_ref))):
            rows = pl.ds(n * some * CX, some * CX)
            loads.append(
                pltpu.make_async_copy(source.at[rows], target.at[rows], sems.at[2 * n + m])
            )
            loads[-1].start()
    none = jnp.zeros((EX, SB), F32)
    for ref in (field, later):
        ref[0] = none
        ref[DZ + 1] = none
    for n in range(CHUNKS):
        loads[2 * n].wait()
        loads[2 * n + 1].wait()
        for z in range(n * some, (n + 1) * some):
            field[z + 1, :CX] = die_ref[z * CX : (z + 1) * CX, :]
            field[z + 1, CX:] = die_rim[z * 8 : (z + 1) * 8, :]
            rate[z, :CX] = diff_ref[z * CX : (z + 1) * CX, :]
            rate[z, CX:] = diff_rim[z * 8 : (z + 1) * 8, :]
    gap = jnp.abs(iota((SB, SB), 0) - iota((SB, SB), 1))
    band = jnp.where(gap == 0, 1.0, jnp.where(gap == 1, 0.5, 0.0)).astype(BF16)

    def around(ref, start):
        layers = []
        for n in range(GROUP):
            z = start + n
            layers.append(2.0 * ref[z + 1] + (ref[z] + ref[z + 2]))
        p = jnp.concatenate(layers, axis=0)
        high, low = split(p)
        q = jnp.dot(high, band, preferred_element_type=F32)
        q = q + jnp.dot(low, band, preferred_element_type=F32)
        for n in range(GROUP):
            own = q[n * EX : (n + 1) * EX]
            yield own + 0.5 * (pltpu.roll(own, 1, 0) + pltpu.roll(own, EX - 1, 0))

    def first(g, carry):
        for n, q in enumerate(around(field, g * GROUP)):
            z = g * GROUP + n
            v = field[z + 1]
            later[z + 1] = v + rate[z] * (q - 16.0 * v)
        return carry

    lax.fori_loop(0, DZ // GROUP, first, 0, unroll=4 * UNROLL)

    def second(g, carry):
        for n, q in enumerate(around(later, g * GROUP)):
            z = g * GROUP + n
            v = later[z + 1, :CX]
            out_ref[z] = v + rate[z, :CX] * (q[:CX] - 16.0 * v)
        return carry

    lax.fori_loop(0, DZ // GROUP, second, 0, unroll=4 * UNROLL)


def smooth(x):
    z = 2.0 * x + (pltpu.roll(x, 2, 1) + pltpu.roll(x, 126, 1))
    return z + 0.5 * (pltpu.roll(z, 1, 0) + pltpu.roll(z, EX - 1, 0))


def finish_kernel(
    base_ref, diff_top, diff_rim, heat_ref, even_own, odd_own, even_in, odd_in, out_hbm,
    out_ref, out_sems,
):
    some = DZ // CHUNKS
    depth_even = lax.rem(lax.axis_index("depth"), 2) == 0
    lane = iota((EX, 128), 1)
    die = lane < 2 * DZ
    first_lane = jnp.logical_and(die, lax.rem(lane, 2) == 0)
    second_lane = jnp.logical_and(die, lax.rem(lane, 2) == 1)

    def parts(even_ref, odd_ref, when):
        v = jnp.where(when, even_ref[:EX, :128], odd_ref[:EX, :128])
        return v, jnp.where(when, even_ref[:EX, 128:], odd_ref[:EX, 128:])

    right_v, right_k = parts(even_own, odd_own, depth_even)
    left_v, left_k = parts(even_own, odd_own, jnp.logical_not(depth_even))
    after_v, after_k = parts(even_in, odd_in, depth_even)
    before_v, before_k = parts(even_in, odd_in, jnp.logical_not(depth_even))

    def up(x):
        return pltpu.roll(x, 1, 1)

    def down(x):
        return pltpu.roll(x, 127, 1)

    def change(own_v, own_k, out_v, out_k, outer, inner, to_outer, to_inner):
        own_w, out_w = smooth(jnp.where(die, own_v, 0.0)), smooth(jnp.where(die, out_v, 0.0))
        near = out_v + out_k * (
            out_w + 0.5 * (to_outer(out_w) + to_outer(own_w)) - 16.0 * out_v
        )
        near = jnp.where(outer, near, 0.0)
        moved = jnp.where(inner, 0.5 * own_k * to_inner(out_w), 0.0)
        spread = smooth(moved)
        edge = moved + own_k * (spread - 16.0 * moved + 0.5 * to_inner(smooth(near)))
        return jnp.where(inner, edge, jnp.where(die, 0.5 * own_k * to_outer(spread), 0.0))

    left = change(left_v, left_k, before_v, before_k, second_lane, first_lane, up, down)
    right = change(right_v, right_k, after_v, after_k, first_lane, second_lane, down, up)

    h_right, h_left = pltpu.roll(after_v, 128 - 2 * DZ, 1), pltpu.roll(before_v, 126 - 2 * DZ, 1)
    rim = jnp.where(lane < 2, h_right, jnp.where(lane >= 126, h_left, 0.0))
    heat = jnp.concatenate([heat_ref[...], rim], axis=1)
    rates = []
    for z in range(3):
        k_right = pltpu.roll(after_k, (128 - 2 * z) % 128, 1)
        k_left = pltpu.roll(before_k, 126 - 2 * z, 1)
        k_rim = jnp.where(lane < 1, k_right, jnp.where(lane >= 127, k_left, 0.0))
        own = jnp.concatenate([diff_top[z], diff_rim[z * 8 : (z + 1) * 8, :]], axis=0)
        rates.append(jnp.concatenate([own, k_rim], axis=1))
    around = across(heat)
    first = heat + rates[0] * (2.0 * around - 16.0 * heat)
    second = rates[1] * around
    added = []
    for rate, own, p in (
        (rates[0], first, 2.0 * first + second),
        (rates[1], second, 2.0 * second + first),
        (rates[2], 0.0, second),
    ):
        added.append((own + rate * (across(p) - 16.0 * own))[:CX, :SB])

    left, right = left[:CX], right[:CX]
    edge = iota((CX, 128), 1)
    stores = []
    for n in range(CHUNKS):
        for z in range(n * some, (n + 1) * some):
            at_left = pltpu.roll(left, (128 - 2 * z) % 128, 1)
            at_right = pltpu.roll(right, 126 - 2 * z, 1)
            near = jnp.where(edge < 2, at_left, 0.0)
            far = jnp.where(edge >= 126, at_right, 0.0)
            step = jnp.concatenate([near, far], axis=1)
            if z < 3:
                step = step + added[z]
            out_ref[z] = base_ref[z] + step
        layers = pl.ds(n * some, some)
        stores.append(
            pltpu.make_async_copy(out_ref.at[layers], out_hbm.at[layers], out_sems.at[n])
        )
        stores[-1].start()
    for store in stores:
        store.wait()


def owner_kernel(
    got_hbm, face_hbm, flux_hbm, heat_hbm, even_hbm, odd_hbm,
    got_ref, face_ref, flux_ref, heat_ref, even_ref, odd_ref, sems, out_sems,
):
    rows = SPAN * PER // PIECES
    loads = [
        pltpu.make_async_copy(
            got_hbm.at[pl.ds(n * rows, rows)], got_ref.at[pl.ds(n * rows, rows)], sems.at[n]
        )
        for n in range(PIECES)
    ]
    loads.append(pltpu.make_async_copy(face_hbm, face_ref, sems.at[PIECES]))
    for load in loads:
        load.start()
    lane = iota((SPAN, 128), 1).astype(F32)
    for load in loads:
        load.wait()
    faces = jnp.concatenate([face_ref[...], jnp.zeros((128 - CX, SB), F32)], axis=0)
    codes = got_ref[pl.ds(4 * CAP, SPAN, stride=PER), :]
    onehot = jnp.concatenate(
        [jnp.where(codes[:, k : k + 1] == lane, 1.0, 0.0) for k in range(CAP)], axis=0
    ).astype(BF16)
    touched = pick(onehot, faces)

    def slots(c):
        return jnp.concatenate(
            [got_ref[pl.ds(k * 4 + c, SPAN, stride=PER), :] for k in range(CAP)], axis=0
        )

    temp = jnp.concatenate([slots(0), slots(1)], axis=1)
    gain = jnp.concatenate([slots(2), slots(3)], axis=1)
    flux = gain * (temp - touched)
    for k in range(CAP):
        for c in range(2):
            flux_ref[pl.ds(c * CAP + k, SPAN, stride=2 * CAP), :] = flux[
                k * SPAN : (k + 1) * SPAN, c * 128 : (c + 1) * 128
            ]
    store = pltpu.make_async_copy(flux_ref, flux_hbm, out_sems.at[3])
    store.start()
    heat = FACE_GAIN * pick(onehot, flux, (((0,), (0,)), ((), ())))[:CX]
    heat_ref[...] = heat
    is_even = lax.rem(lax.axis_index("span"), 2) == 0
    even_ref[...] = jnp.where(is_even, heat[CX - 8 :], heat[:8])
    odd_ref[...] = jnp.where(is_even, heat[:8], heat[CX - 8 :])
    small = [
        pltpu.make_async_copy(source, target, out_sems.at[n])
        for n, (source, target) in enumerate(
            ((heat_ref, heat_hbm), (even_ref, even_hbm), (odd_ref, odd_hbm))
        )
    ]
    for copy in small:
        copy.start()
    for copy in small:
        copy.wait()
    store.wait()


def heat_edges_kernel(
    heat_ref, even_in, odd_in, even_packed, odd_packed, rows_ref, even_ref, odd_ref
):
    span_even = lax.rem(lax.axis_index("span"), 2) == 0
    depth_even = lax.rem(lax.axis_index("depth"), 2) == 0
    below = jnp.where(span_even, even_in[...], odd_in[...])
    above = jnp.where(span_even, odd_in[...], even_in[...])
    sub = iota((8, SB), 0)
    rim = jnp.where(sub < 2, below, jnp.where(sub >= 6, above, 0.0))
    rows = jnp.concatenate([heat_ref[...], rim], axis=0)
    rows_ref[...] = rows
    here = lax.shift_right_logical(iota((EX, 128), 1), 1) == DZ
    left = pltpu.roll(rows[:, :128], 2 * DZ, 1)
    right = pltpu.roll(rows[:, 128:], 2 * DZ + 2, 1)
    for packed, out, one, other in (
        (even_packed, even_ref, right, left),
        (odd_packed, odd_ref, left, right),
    ):
        edge = jnp.where(depth_even, one, other)
        out[:EX, :128] = jnp.where(here, edge, packed[:EX, :128])
        out[:EX, 128:] = packed[:EX, 128:]
        out[EX:, :] = packed[EX:, :]


def shell_kernel(
    routes_ref, temp_ref, even_in, odd_in, flux_hbm, out_ref, flux_ref, sems
):
    some = SPAN // PIECES
    loads = [
        pltpu.make_async_copy(
            flux_hbm.at[pl.ds(n * some, some)], flux_ref.at[pl.ds(n * some, some)], sems.at[n]
        )
        for n in range(PIECES)
    ]
    for load in loads:
        load.start()
    depth_even = lax.rem(lax.axis_index("depth"), 2) == 0
    below = jnp.where(depth_even, even_in[EX : EX + 1, :], odd_in[EX : EX + 1, :])
    above = jnp.where(depth_even, odd_in[EX : EX + 1, :], even_in[EX : EX + 1, :])
    temp = temp_ref[...]
    sub, lane = iota((NB, SB), 0), iota((NB, SB), 1)
    upper = jnp.where(sub == 0, above, pltpu.roll(temp, 1, 0))
    lower = jnp.where(sub == NB - 1, below, pltpu.roll(temp, NB - 1, 0))
    before = jnp.where(lane == 0, 0.0, pltpu.roll(temp, 1, 1))
    after = jnp.where(lane == SB - 1, 0.0, pltpu.roll(temp, SB - 1, 1))
    laplace = lower + upper + after + before - 4.0 * temp
    out_ref[...] = temp + SHELL_RATE * laplace
    target = routes_ref[...].astype(F32)
    target_col = as_column(target, sub == lane)
    same = jnp.logical_and(target_col == target, lane < sub)
    rank_col = jnp.sum(jnp.where(same, 1.0, 0.0), axis=1, keepdims=True)
    position = (target_col * CAP + rank_col).astype(jnp.int32)
    slots = SLOTS // PIECES
    total = jnp.zeros((NB, SB), F32)
    for n in range(PIECES):
        take = jnp.where(iota((NB, slots), 1) + n * slots == position, 1.0, 0.0).astype(BF16)
        loads[n].wait()
        rows = slice(n * some, (n + 1) * some)
        flux = jnp.concatenate(
            [
                flux_ref[rows, c * CAP : (c + 1) * CAP, :].reshape(slots, 128)
                for c in range(2)
            ],
            axis=1,
        )
        total = total + pick(take, flux)
    out_ref[...] -= SHELL_SINK * total


def swap(even, odd, axis):
    size = lax.axis_size(axis)
    pairs = [(i, i ^ 1) for i in range(size)]
    shifted = [(i, ((i + 1) ^ 1) - 1) for i in range(1, size - 1)]
    return lax.ppermute(even, axis, pairs), lax.ppermute(odd, axis, shifted)


def local(shell_temp, contact_gain, die_temp, diffusivity, routes, tile_rows, closed):
    temp, gain = shell_temp[0], contact_gain[0]
    target = routes.reshape(1, NB)
    die, diff = die_temp.reshape(DZ * CX, SB), diffusivity.reshape(DZ * CX, SB)
    rows = jax.ShapeDtypeStruct((3 * DZ, SB), F32)
    even, odd = pl.pallas_call(
        edge_rows_kernel,
        out_shape=(rows, rows),
        grid=(1,),
        in_specs=[
            pl.BlockSpec((DZ, 8, SB), lambda i: (0, 0, 0)),
            pl.BlockSpec((DZ, 8, SB), lambda i: (0, CX // 8 - 1, 0)),
        ]
        * 2,
        out_specs=(VMEM,) * 2,
        compiler_params=params(60),
        name="edge_rows",
    )(die_temp, die_temp, diffusivity, diffusivity)
    sent = pl.pallas_call(
        pack_kernel,
        out_shape=pltpu.HBM((SPAN * PER, 128), F32),
        in_specs=[HBM] * 5,
        out_specs=HBM,
        scratch_shapes=[
            pltpu.VMEM((1, NB), jnp.int32),
            pltpu.VMEM((1, NB), jnp.int32),
            pltpu.VMEM((1, NB), jnp.int32),
            pltpu.VMEM((NB, SB), F32),
            pltpu.VMEM((NB, SB), F32),
            pltpu.VMEM((SPAN * PER, 128), F32),
            pltpu.SemaphoreType.DMA((5,)),
            pltpu.SemaphoreType.DMA((CHUNKS,)),
        ],
        compiler_params=params(60),
        cost_estimate=cost(6 * SLOTS * NB * 2 * SB, 4 * 2**20),
        name="pack",
    )(target, tile_rows, closed, temp, gain)
    got = lax.all_to_all(
        sent.reshape(SPAN * PER, 1, 128), "span", split_axis=0, concat_axis=0, tiled=True
    ).reshape(SPAN * PER, 128)
    even, odd = swap(even, odd, "span")
    columns, rim = pltpu.HBM((EX + 8, SB), F32), pltpu.HBM((DZ * 8, SB), F32)
    even_packed, odd_packed, die_rim, diff_rim, face = pl.pallas_call(
        edge_columns_kernel,
        out_shape=(columns, columns, rim, rim, pltpu.HBM((CX, SB), F32)),
        grid=(1,),
        in_specs=[VMEM] * 5,
        out_specs=(whole(EX + 8, SB),) * 2 + (whole(DZ * 8, SB),) * 2 + (whole(CX, SB),),
        compiler_params=params(16),
        name="edge_columns",
    )(die, diff, even, odd, temp)

    edge = pltpu.HBM((8, SB), F32)
    flux, heat, even, odd = pl.pallas_call(
        owner_kernel,
        out_shape=(
            pltpu.HBM((2 * SLOTS, 128), F32),
            pltpu.HBM((CX, SB), F32),
            edge,
            edge,
        ),
        grid=(1,),
        in_specs=[HBM] * 2,
        out_specs=(HBM,) * 4,
        scratch_shapes=[
            pltpu.VMEM((SPAN * PER, 128), F32),
            pltpu.VMEM((CX, SB), F32),
            pltpu.VMEM((2 * SLOTS, 128), F32),
            pltpu.VMEM((CX, SB), F32),
            pltpu.VMEM((8, SB), F32),
            pltpu.VMEM((8, SB), F32),
            pltpu.SemaphoreType.DMA((PIECES + 1,)),
            pltpu.SemaphoreType.DMA((4,)),
        ],
        compiler_params=params(60),
        name="owner",
    )(got, face)
    back = lax.all_to_all(
        flux.reshape(SPAN, 2 * CAP, 128), "span", split_axis=0, concat_axis=0, tiled=True
    )
    even, odd = swap(even, odd, "span")
    heat_rows, even, odd = pl.pallas_call(
        heat_edges_kernel,
        out_shape=(jax.ShapeDtypeStruct((EX, SB), F32),)
        + (jax.ShapeDtypeStruct((EX + 8, SB), F32),) * 2,
        in_specs=[VMEM] * 5,
        out_specs=(VMEM,) * 3,
        compiler_params=params(8),
        cost_estimate=cost(10**12, 2**32),
        name="heat_edges",
    )(heat, even, odd, even_packed, odd_packed)
    base = pl.pallas_call(
        sweeps_kernel,
        out_shape=jax.ShapeDtypeStruct((DZ, CX, SB), F32),
        grid=(1,),
        in_specs=[HBM, HBM, whole(DZ * 8, SB), whole(DZ * 8, SB), VMEM],
        out_specs=VMEM,
        scratch_shapes=[
            pltpu.VMEM((DZ * CX, SB), F32),
            pltpu.VMEM((DZ * CX, SB), F32),
            pltpu.VMEM((DZ + 2, EX, SB), F32),
            pltpu.VMEM((DZ + 2, EX, SB), F32),
            pltpu.VMEM((DZ, EX, SB), F32),
            pltpu.SemaphoreType.DMA((2 * CHUNKS,)),
        ],
        compiler_params=params(24),
        name="sweeps",
    )(die, diff, die_rim, diff_rim, heat_rows)
    even_own, odd_own = even, odd
    even, odd = swap(even, odd, "depth")
    die_next = pl.pallas_call(
        finish_kernel,
        out_shape=pltpu.HBM((DZ, CX, SB), F32),
        grid=(1,),
        in_specs=[
            VMEM,
            whole(3, CX, SB),
            pl.BlockSpec((24, SB), lambda i: (0, 0)),
        ]
        + [VMEM] * 5,
        out_specs=HBM,
        scratch_shapes=[
            pltpu.VMEM((DZ, CX, SB), F32),
            pltpu.SemaphoreType.DMA((CHUNKS,)),
        ],
        compiler_params=params(16),
        name="finish",
    )(base, diffusivity, diff_rim, heat_rows, even_own, odd_own, even, odd)
    shell_next = pl.pallas_call(
        shell_kernel,
        out_shape=pltpu.HBM((NB, SB), F32),
        grid=(1,),
        in_specs=[VMEM, VMEM, VMEM, VMEM, HBM],
        out_specs=whole(NB, SB),
        scratch_shapes=[
            pltpu.VMEM((SPAN, 2 * CAP, 128), F32),
            pltpu.SemaphoreType.DMA((PIECES,)),
        ],
        compiler_params=params(16),
        name="shell",
    )(target, temp, even, odd, back)
    return shell_next[None], die_next


def solution(mesh):
    placed = (
        P("span", "depth", None),
        P("span", "depth", None),
        P(None, "span", "depth"),
        P(None, "span", "depth"),
        P("span", "depth", None),
        P("span", "depth"),
        P("span", "depth"),
    )
    return jax.shard_map(
        local,
        mesh=mesh,
        in_specs=placed,
        out_specs=(P("span", "depth", None), P(None, "span", "depth")),
        check_vma=False,
    )
```
